256 devices in a mesh: cell: 32 (over z, y), view: 8 (over x, core).
Axes of the slice: x: 4, y: 4, z: 8, core: 2. Of those that a mesh axis runs over, the one named last changes fastest.
Arguments:
- gaussians: float32 [59, 1048576], P(None, 'cell'), may hold values from -256 to 256
- cameras: float32 [8, 7], P('view'), may hold values from -1 to 1.005
- fetch_ids: int32 [32, 32, 128], P('cell'), may hold values from 0 to 32767, as said below
- tile_lists: int32 [8, 256, 512], P('view', 'cell'), may hold values from 0 to 4095, as said below
- lengths: int32 [256], P('cell'), may hold values from 128 to 512, as said below
- target_image: float32 [3, 8, 256, 256], P(None, 'view', 'cell'), may hold values from 0 to 1
Outputs:
- rendered: float32 [3, 8, 256, 256], P(None, 'view', 'cell')
- param_grads: float32 [59, 1048576], P(None, ('cell', 'view'))
The draws below stay inside these ranges and needn't reach their ends.
Inputs may be any that keep to these rules, and one draw needn't show every extreme that they name: Each row fetch_ids[c, o] holds 128 distinct local indices of owner cell o, and no index stands under two requesting cells. `tile_lists`: A value o * 128 + s names slot s of owner cell o in the fetch_ids row of the tile's cell (t // 8). The first lengths[t] entries of a tile are distinct; the rest are ignored. `lengths`: on every index of cell some tile has 512 live entries.
All inputs are finite; a program needn't handle non-finite values.
Results may differ from the reference program's by a relative error of at most 0.0003.
Values sent between devices are 32-bit elements; how exact they have to be, the bound alone decides.
A program may use at most 128 MiB of HBM per device.

```python
import jax
import jax.numpy as jnp
from jax import lax

PIXELS = 256
LIST = 512
TILES_DEV = 8
GAUSS_DEV = 32768
CELLS = 32
VIEWS = 8
TILES = 256
CAP = 128


def plan_rows(key):
    key_lens, key_force, key_hot, key_weight, key_noise, key_fill = jax.random.split(key, 6)
    slot_count = CELLS * CAP
    live_lens = jax.random.randint(key_lens, (TILES_DEV,), LIST // 4, LIST + 1)
    forced = jax.random.randint(key_force, (), 0, TILES_DEV)
    live_lens = jnp.where(jnp.arange(TILES_DEV) == forced, LIST, live_lens).astype(jnp.int32)
    owner_of = jnp.arange(slot_count, dtype=jnp.int32) // CAP
    hottest = jax.random.randint(key_hot, (), 0, CELLS)
    weights = jax.random.randint(key_weight, (CELLS,), 0, CELLS)
    noise = jax.random.randint(key_noise, (slot_count,), 0, 2 * CAP)
    score = jnp.where(owner_of == hottest, -1, weights[owner_of] * (CAP // 2 + 1) + noise)
    ranking = jnp.argsort(score, stable=True).astype(jnp.int32)
    ends = jnp.cumsum(live_lens).astype(jnp.int32)
    starts = ends - live_lens
    within = jnp.arange(LIST, dtype=jnp.int32)
    picked = jnp.minimum(starts[:, None] + within[None, :], slot_count - 1)
    live_mask = within[None, :] < live_lens[:, None]
    filler = jax.random.randint(key_fill, (TILES_DEV, LIST), 0, slot_count)
    listed = jnp.where(live_mask, ranking[picked], filler).astype(jnp.int32)
    rank_of = jnp.zeros((slot_count,), jnp.int32).at[ranking].set(jnp.arange(slot_count, dtype=jnp.int32))
    tile_of = jnp.sum((rank_of[:, None] >= ends[None, :]).astype(jnp.int32), axis=1)
    return (live_lens, listed, live_mask, tile_of)


def fetch_plan(key):
    key = jax.random.fold_in(key, 7)
    key_rows, key_perm = jax.random.split(key)
    live_lens, listed, live_mask, tile_of = jax.vmap(plan_rows)(jax.random.split(key_rows, CELLS))
    perms = jax.vmap(lambda one_key: jax.random.permutation(one_key, GAUSS_DEV))(jax.random.split(key_perm, CELLS)).astype(jnp.int32)
    fetch = jnp.transpose(perms[:, :CELLS * CAP].reshape(CELLS, CELLS, CAP), (1, 0, 2))
    cell_base = (jnp.arange(CELLS, dtype=jnp.int32) * TILES_DEV)[:, None]
    home_tile = jnp.where(tile_of < TILES_DEV, cell_base + tile_of, -1).reshape(CELLS, CELLS, CAP)
    owner_index = jnp.broadcast_to(jnp.arange(CELLS, dtype=jnp.int32)[None, :, None], fetch.shape)
    homes = jnp.full((CELLS, GAUSS_DEV), -1, jnp.int32).at[owner_index, fetch].set(home_tile)
    return (fetch, live_lens, listed, live_mask, homes)


def draw_fetch_ids(key, part):
    return fetch_plan(key)[0]


def draw_lengths(key, part):
    return fetch_plan(key)[1].reshape(TILES).astype(jnp.int32)


def draw_tile_lists(key, part):
    plan = fetch_plan(key)
    listed, live_mask = (plan[2], plan[3])
    key = jax.random.fold_in(key, 11)
    depth = jax.random.randint(key, (VIEWS, CELLS, TILES_DEV, LIST), 0, 4 * LIST)
    within = jnp.arange(LIST, dtype=jnp.int32)
    depth = jnp.where(live_mask[None], depth, 4 * LIST + within)
    ordering = jnp.argsort(depth, axis=-1, stable=True)
    ordered = jnp.take_along_axis(jnp.broadcast_to(listed[None], depth.shape), ordering, axis=-1)
    return ordered.reshape(VIEWS, TILES, LIST).astype(jnp.int32)


def draw_gaussians(key, part):
    homes = fetch_plan(key)[4].reshape(CELLS * GAUSS_DEV)
    key = jax.random.fold_in(key, 13)
    keys = jax.random.split(key, 8)
    total = CELLS * GAUSS_DEV
    height = 2.0 * TILES
    placed = homes >= 0
    column = (jnp.maximum(homes, 0) % 8).astype(jnp.float32)
    row_index = (jnp.maximum(homes, 0) // 8).astype(jnp.float32)
    jitter = jax.random.uniform(keys[0], (2, total), jnp.float32, 4.0, 12.0)
    spread_x = jax.random.uniform(keys[1], (total,), jnp.float32, -64.0, 64.0)
    spread_y = jax.random.uniform(keys[2], (total,), jnp.float32, -0.5 * height, 0.5 * height)
    coord_x = jnp.where(placed, column * 16.0 + jitter[0] - 64.0, spread_x)
    coord_y = jnp.where(placed, row_index * 16.0 + jitter[1] - 0.5 * height, spread_y)
    coord_z = jax.random.uniform(keys[3], (total,), jnp.float32, -3.0, 3.0)
    log_scales = jax.random.uniform(keys[4], (3, total), jnp.float32, -0.69, 0.47)
    coef_scale = jnp.where(jnp.arange(48) < 3, 0.8, 0.5).astype(jnp.float32)[:, None]
    quaternion = jnp.clip(jax.random.normal(keys[5], (4, total), jnp.float32), -4.0, 4.0)
    coefficients = jnp.clip(jax.random.normal(keys[6], (48, total), jnp.float32), -4.0, 4.0) * coef_scale
    flags = jax.random.uniform(keys[7], (2, total), jnp.float32)
    logits = jnp.where(flags[0] < 0.06, 4.7 + 0.8 * flags[1], -5.0 + 4.0 * flags[1])
    return jnp.concatenate([coord_x[None], coord_y[None], coord_z[None], log_scales, quaternion, logits[None], coefficients], axis=0)


def draw_cameras(key, part):
    key = jax.random.fold_in(key, 17)
    lowest = jnp.array([-0.01, -0.1, -0.1, -1.0, -1.0, 0.995, 0.995], jnp.float32)
    highest = jnp.array([0.01, 0.1, 0.1, 1.0, 1.0, 1.005, 1.005], jnp.float32)
    unit = jax.random.uniform(key, (VIEWS, 7), jnp.float32)
    return lowest + (highest - lowest) * unit


def level_of(rng, dims, shards, low, high):
    def one(dim, shards_of):
        steps = jax.random.uniform(jax.random.fold_in(jax.random.fold_in(rng, 6), dim), (shards_of,), jnp.float32, low / len(shards), high / len(shards))
        return jnp.repeat(jnp.exp(steps), dims[dim] // shards_of).reshape((-1,) + (1,) * (len(dims) - dim - 1))

    loudness = one(*shards[0])
    for cut in shards[1:]:
        loudness = loudness * one(*cut)
    return loudness


def setup_inputs(seed: int = 0) -> dict:
    key_list = jax.random.split(jax.random.key(seed), 7)
    return {
        "gaussians": draw_gaussians(jax.random.fold_in(key_list[6], 71), 0),
        "cameras": draw_cameras(jax.random.fold_in(key_list[6], 71), 0),
        "fetch_ids": draw_fetch_ids(jax.random.fold_in(key_list[6], 71), 0),
        "tile_lists": draw_tile_lists(jax.random.fold_in(key_list[6], 71), 0),
        "lengths": draw_lengths(jax.random.fold_in(key_list[6], 71), 0),
        "target_image": jnp.clip(1.0 * jax.random.uniform(key_list[5], (3, VIEWS, TILES, PIXELS), jnp.float32) ** level_of(key_list[5], (3, VIEWS, TILES, PIXELS), ((1, 8), (2, 32)), -0.2, 0.2), 0.0, 1.0),
    }


harmonic_zero = 0.28209479177387814
harmonic_one = 0.4886025119029199
harmonic_two = (1.0925484305920792, -1.0925484305920792, 0.31539156525252005, -1.0925484305920792, 0.5462742152960396)
harmonic_three = (-0.5900435899266435, 2.890611442640554, -0.4570457994644658, 0.3731763325901154, -0.4570457994644658, 1.445305721320277, -0.5900435899266435)

def harmonic_basis(direction):
    along_x, along_y, along_z = (direction[0], direction[1], direction[2])
    square_x, square_y, square_z = (along_x * along_x, along_y * along_y, along_z * along_z)
    terms = [harmonic_zero + 0.0 * along_x, -harmonic_one * along_y, harmonic_one * along_z, -harmonic_one * along_x, harmonic_two[0] * along_x * along_y, harmonic_two[1] * along_y * along_z, harmonic_two[2] * (2.0 * square_z - square_x - square_y), harmonic_two[3] * along_x * along_z, harmonic_two[4] * (square_x - square_y), harmonic_three[0] * along_y * (3.0 * square_x - square_y), harmonic_three[1] * along_x * along_y * along_z, harmonic_three[2] * along_y * (4.0 * square_z - square_x - square_y), harmonic_three[3] * along_z * (2.0 * square_z - 3.0 * square_x - 3.0 * square_y), harmonic_three[4] * along_x * (4.0 * square_z - square_x - square_y), harmonic_three[5] * along_z * (square_x - square_y), harmonic_three[6] * along_x * (square_x - 3.0 * square_y)]
    return jnp.stack(terms)

def camera_rotation(camera):
    cos_yaw, sin_yaw = (jnp.cos(camera[0]), jnp.sin(camera[0]))
    cos_pitch, sin_pitch = (jnp.cos(camera[1]), jnp.sin(camera[1]))
    cos_roll, sin_roll = (jnp.cos(camera[2]), jnp.sin(camera[2]))
    return [[cos_yaw * cos_pitch, cos_yaw * sin_pitch * sin_roll - sin_yaw * cos_roll, cos_yaw * sin_pitch * cos_roll + sin_yaw * sin_roll], [sin_yaw * cos_pitch, sin_yaw * sin_pitch * sin_roll + cos_yaw * cos_roll, sin_yaw * sin_pitch * cos_roll - cos_yaw * sin_roll], [-sin_pitch, cos_pitch * sin_roll, cos_pitch * cos_roll]]

def project(values, camera, height):
    rotation = camera_rotation(camera)
    position = values[0:3]
    across = rotation[0][0] * position[0] + rotation[0][1] * position[1] + rotation[0][2] * position[2]
    upward = rotation[1][0] * position[0] + rotation[1][1] * position[1] + rotation[1][2] * position[2]
    screen_u = camera[5] * across + 64.0 + camera[3]
    screen_v = camera[6] * upward + 0.5 * height + camera[4]
    scales = jnp.exp(values[3:6])
    quaternion = values[6:10]
    magnitude = jnp.maximum(jnp.sqrt(lax.optimization_barrier(jnp.sum(quaternion * quaternion, axis=0))), 0.5)
    real_part = quaternion[0] / magnitude
    imag_x = quaternion[1] / magnitude
    imag_y = quaternion[2] / magnitude
    imag_z = quaternion[3] / magnitude
    turned = [[1.0 - 2.0 * (imag_y * imag_y + imag_z * imag_z), 2.0 * (imag_x * imag_y - real_part * imag_z), 2.0 * (imag_x * imag_z + real_part * imag_y)], [2.0 * (imag_x * imag_y + real_part * imag_z), 1.0 - 2.0 * (imag_x * imag_x + imag_z * imag_z), 2.0 * (imag_y * imag_z - real_part * imag_x)], [2.0 * (imag_x * imag_z - real_part * imag_y), 2.0 * (imag_y * imag_z + real_part * imag_x), 1.0 - 2.0 * (imag_x * imag_x + imag_y * imag_y)]]
    first_row = [camera[5] * (rotation[0][0] * turned[0][col] + rotation[0][1] * turned[1][col] + rotation[0][2] * turned[2][col]) * scales[col] for col in range(3)]
    second_row = [camera[6] * (rotation[1][0] * turned[0][col] + rotation[1][1] * turned[1][col] + rotation[1][2] * turned[2][col]) * scales[col] for col in range(3)]
    sigma_uu = first_row[0] * first_row[0] + first_row[1] * first_row[1] + first_row[2] * first_row[2] + 0.3
    sigma_uv = first_row[0] * second_row[0] + first_row[1] * second_row[1] + first_row[2] * second_row[2]
    sigma_vv = second_row[0] * second_row[0] + second_row[1] * second_row[1] + second_row[2] * second_row[2] + 0.3
    determinant = sigma_uu * sigma_vv - sigma_uv * sigma_uv
    opacity = jax.nn.sigmoid(values[10])
    harmonics = harmonic_basis(jnp.stack(rotation[2]))
    coefficients = values[11:59].reshape(16, 3, values.shape[1])
    colors = 0.5 + lax.optimization_barrier(jnp.sum(harmonics[:, None, None] * coefficients, axis=0))
    return jnp.stack([screen_u, screen_v, sigma_vv / determinant, -sigma_uv / determinant, sigma_uu / determinant, opacity, colors[0], colors[1], colors[2]])

def render(features, live_count, tile_index):
    list_len = features.shape[1]
    pixel_index = jnp.arange(256, dtype=jnp.int32)
    pixel_u = (tile_index % 8 * 16 + pixel_index % 16).astype(jnp.float32) + 0.5
    pixel_v = (tile_index // 8 * 16 + pixel_index // 16).astype(jnp.float32) + 0.5
    offset_u = pixel_u[None, :] - features[0][:, None]
    offset_v = pixel_v[None, :] - features[1][:, None]
    power = -0.5 * (features[2][:, None] * offset_u * offset_u + 2.0 * features[3][:, None] * offset_u * offset_v + features[4][:, None] * offset_v * offset_v)
    active = (jnp.arange(list_len, dtype=jnp.int32) < live_count)[:, None]
    alpha = jnp.where(active, jnp.minimum(features[5][:, None] * jnp.exp(power), 0.99), 0.0)
    log_keep = jnp.log(1.0 - alpha)
    before = jnp.cumsum(log_keep, axis=0) - log_keep
    weight = jnp.exp(before) * alpha
    return jnp.dot(features[6:9], weight, precision=lax.Precision.HIGHEST)

def reference(gaussians, cameras, fetch_ids, tile_lists, lengths, target_image):
    height = 2.0 * TILES
    owner_base = (jnp.arange(CELLS, dtype=jnp.int32) * GAUSS_DEV)[None, :, None]
    slot_table = (owner_base + fetch_ids).reshape(CELLS, CELLS * CAP)
    tile_ids = jnp.arange(TILES, dtype=jnp.int32)
    shard_of = tile_ids // TILES_DEV
    gradient = jnp.zeros(gaussians.shape, jnp.float32)
    pictures = []
    for view_index in range(VIEWS):
        camera = cameras[view_index]
        global_ids = slot_table[shard_of[:, None], tile_lists[view_index]]
        goal_pixels = jnp.transpose(target_image[:, view_index], (1, 0, 2))

        def view_loss(values):
            features = project(values, camera, height)

            def one_tile(items):
                tile_index, chosen, live_count, goal = items
                image = render(jnp.take(features, chosen, axis=1), live_count, tile_index)
                return (image, 0.5 * jnp.sum((image - goal) ** 2))
            images, losses = lax.map(jax.checkpoint(one_tile), (tile_ids, global_ids, lengths, goal_pixels))
            return (jnp.sum(losses), images)
        loss_value, pull_back, images = jax.vjp(view_loss, gaussians, has_aux=True)
        gradient = gradient + pull_back(jnp.ones((), jnp.float32))[0]
        pictures.append(jnp.transpose(images, (1, 0, 2)))
    return (jnp.stack(pictures, axis=1), gradient)
```

```python
import functools

import jax
import jax.numpy as jnp
import numpy as np
from jax import lax
from jax.experimental import pallas as pl
from jax.experimental.pallas import tpu as pltpu
from jax.sharding import PartitionSpec as P

MESH = pl.DeviceIdType.MESH
LOG2E = 1.4426950408889634
F32 = jnp.float32
BF16 = jnp.bfloat16

harmonic_zero = 0.28209479177387814
harmonic_one = 0.4886025119029199
harmonic_two = (
    1.0925484305920792,
    -1.0925484305920792,
    0.31539156525252005,
    -1.0925484305920792,
    0.5462742152960396,
)
harmonic_three = (
    -0.5900435899266435,
    2.890611442640554,
    -0.4570457994644658,
    0.3731763325901154,
    -0.4570457994644658,
    1.445305721320277,
    -0.5900435899266435,
)


def harmonic_basis(direction):
    along_x, along_y, along_z = (direction[0], direction[1], direction[2])
    square_x, square_y, square_z = (along_x * along_x, along_y * along_y, along_z * along_z)
    return [
        harmonic_zero + 0.0 * along_x,
        -harmonic_one * along_y,
        harmonic_one * along_z,
        -harmonic_one * along_x,
        harmonic_two[0] * along_x * along_y,
        harmonic_two[1] * along_y * along_z,
        harmonic_two[2] * (2.0 * square_z - square_x - square_y),
        harmonic_two[3] * along_x * along_z,
        harmonic_two[4] * (square_x - square_y),
        harmonic_three[0] * along_y * (3.0 * square_x - square_y),
        harmonic_three[1] * along_x * along_y * along_z,
        harmonic_three[2] * along_y * (4.0 * square_z - square_x - square_y),
        harmonic_three[3] * along_z * (2.0 * square_z - 3.0 * square_x - 3.0 * square_y),
        harmonic_three[4] * along_x * (4.0 * square_z - square_x - square_y),
        harmonic_three[5] * along_z * (square_x - square_y),
        harmonic_three[6] * along_x * (square_x - 3.0 * square_y),
    ]


def camera_columns(cams):
    cosine, sine = jnp.cos(cams), jnp.sin(cams)
    wide = lambda t, k: jnp.broadcast_to(t[:, k:k + 1], (8, 128))
    cos_yaw, cos_pitch, cos_roll = [wide(cosine, k) for k in range(3)]
    sin_yaw, sin_pitch, sin_roll = [wide(sine, k) for k in range(3)]
    shift_u, shift_v, scale_u, scale_v = [wide(cams, k) for k in range(3, 7)]
    first = [
        cos_yaw * cos_pitch,
        cos_yaw * sin_pitch * sin_roll - sin_yaw * cos_roll,
        cos_yaw * sin_pitch * cos_roll + sin_yaw * sin_roll,
    ]
    second = [
        sin_yaw * cos_pitch,
        sin_yaw * sin_pitch * sin_roll + cos_yaw * cos_roll,
        sin_yaw * sin_pitch * cos_roll - cos_yaw * sin_roll,
    ]
    third = [-sin_pitch, cos_pitch * sin_roll, cos_pitch * cos_roll]
    return (
        [scale_u * t for t in first] + [64.0 + shift_u]
        + [scale_v * t for t in second] + [256.0 + shift_v]
        + harmonic_basis(third)
    )


def place():
    cell, view = lax.axis_index("cell"), lax.axis_index("view")
    return cell, view, cell >> 2, cell & 3, view >> 1, view & 1


def requester(i, z, y, x, core):
    dz = core + 2 * i
    return (((z + dz) & 7) << 2) | ((y + x - dz) & 3)


def server(i, z, y, x, core):
    dz = core + 2 * i
    return (((z - dz) & 7) << 2) | ((y - x + dz) & 3)


def greet():
    cell, view, z, y, x, core = place()
    barrier = pltpu.get_barrier_semaphore()

    def signal(where, who):
        pl.semaphore_signal(barrier, inc=1, device_id=(where, who), device_id_type=MESH)

    for i in range(4):
        if i == 0:
            @pl.when(view != 0)
            def _():
                signal(requester(0, z, y, x, core), view)
                signal(server(0, z, y, x, core), view)
        else:
            signal(requester(i, z, y, x, core), view)
            signal(server(i, z, y, x, core), view)
    for step in range(1, 8):
        signal(cell, (view + step) & 7)
    pl.semaphore_wait(barrier, jnp.where(view == 0, 13, 15))


class Or_local:
    def __init__(self, i, view, remote, local):
        self.first, self.view, self.remote, self.local = i == 0, view, remote, local

    def each(self, remote_act, local_act):
        if not self.first:
            remote_act(self.remote())
            return

        if local_act is not None:
            @pl.when(self.view == 0)
            def _():
                local_act(self.local())

        @pl.when(self.view != 0)
        def _():
            remote_act(self.remote())

    def start(self):
        self.each(lambda c: c.start(), lambda c: c.start())

    def wait_recv(self):
        self.each(lambda c: c.wait_recv(), lambda c: c.wait())

    def wait_send(self):
        self.each(lambda c: c.wait_send(), None)


def remote(source, target, send, recv, where, who):
    return pltpu.make_async_remote_copy(
        src_ref=source, dst_ref=target, send_sem=send, recv_sem=recv,
        device_id=(where, who), device_id_type=MESH,
    )


def rotation_of(values):
    scales = [jnp.exp(values[3 + k]) for k in range(3)]
    norm = jnp.sqrt(
        values[6] * values[6] + values[7] * values[7] + values[8] * values[8] + values[9] * values[9]
    )
    inverse = 1.0 / jnp.maximum(norm, 0.5)
    qw, qx, qy, qz = [values[6 + k] * inverse for k in range(4)]
    turned = [
        [1.0 - 2.0 * (qy * qy + qz * qz), 2.0 * (qx * qy - qw * qz), 2.0 * (qx * qz + qw * qy)],
        [2.0 * (qx * qy + qw * qz), 1.0 - 2.0 * (qx * qx + qz * qz), 2.0 * (qy * qz - qw * qx)],
        [2.0 * (qx * qz - qw * qy), 2.0 * (qy * qz + qw * qx), 1.0 - 2.0 * (qx * qx + qy * qy)],
    ]
    return scales, (qw, qx, qy, qz), norm, inverse, turned


def conic_of(consts, scaled):
    first = [sum(consts[r] * scaled[r][k] for r in range(3)) for k in range(3)]
    second = [sum(consts[4 + r] * scaled[r][k] for r in range(3)) for k in range(3)]
    uu = first[0] * first[0] + first[1] * first[1] + first[2] * first[2] + 0.3
    uv = first[0] * second[0] + first[1] * second[1] + first[2] * second[2]
    vv = second[0] * second[0] + second[1] * second[1] + second[2] * second[2] + 0.3
    det = uu * vv - uv * uv
    return vv / det, -uv / det, uu / det


def log_sigmoid(x):
    return jnp.minimum(x, 0.0) - jnp.log(1.0 + jnp.exp(-jnp.abs(x)))


def ask_kernel(
    cam_ref, fetch_ref, ids_out, cams_out,
    row, cams, idv, loc_sem, id_send, id_recv, cam_send, cam_recv,
):
    cell, view, z, y, x, core = place()
    row[...] = jnp.zeros_like(row)
    row[:, 0:7] = cam_ref[...]
    greet()

    def id_copy(i):
        owner = server(i, z, y, x, core)
        source, target = fetch_ref.at[pl.ds(owner, 1)], idv.at[pl.ds(i, 1)]
        return Or_local(
            i, view,
            lambda: remote(source, target, id_send.at[i], id_recv.at[i], owner, view),
            lambda: pltpu.make_async_copy(source, target, id_recv.at[i]),
        )

    def cam_copy(step):
        return remote(
            row, cams.at[pl.ds(view, 1)], cam_send.at[step], cam_recv.at[step],
            cell, (view + step) & 7,
        )

    for i in range(4):
        id_copy(i).start()
    for step in range(1, 8):
        cam_copy(step).start()
    mine = pltpu.make_async_copy(row, cams.at[pl.ds(view, 1)], loc_sem)
    mine.start()
    for i in range(4):
        id_copy(i).wait_recv()
    ids_out[...] = idv[...]
    for step in range(1, 8):
        cam_copy(step).wait_recv()
    mine.wait()
    cams_out[...] = cams[...]
    for i in range(4):
        id_copy(i).wait_send()
    for step in range(1, 8):
        cam_copy(step).wait_send()


def project_kernel(
    ids_ref, cams_ref, gauss_ref, feat_out, params_out, consts_out, tab, got, sem,
):
    cell, view, z, y, x, core = place()
    whole = pltpu.make_async_copy(gauss_ref, tab, sem)
    whole.start()
    consts = camera_columns(cams_ref[...])
    lanes = lax.broadcasted_iota(jnp.int32, (8, 128), 1)
    packed = jnp.zeros((8, 128), F32)
    for k in range(24):
        packed = jnp.where(lanes == k, consts[k], packed)
    consts_out[...] = packed
    lane = lax.broadcasted_iota(jnp.int32, (59, 128), 1)
    whole.wait()

    def serve(i, carry):
        acc = jnp.zeros((59, 128), F32)
        for n in range(128):
            name = ids_ref[i, n]
            block = tab[:, pl.ds(pl.multiple_of((name >> 7) << 7, 128), 128)]
            acc = jnp.where(lane == n, pltpu.roll(block, (n - name) & 127, 1), acc)
        got[0:59] = acc
        params_out[i] = got[0:16]
        values = [got[k:k + 1] for k in range(59)]
        served = requester(i, z, y, x, core)
        screen_u = sum(consts[r] * values[r] for r in range(3)) + consts[3]
        screen_v = sum(consts[4 + r] * values[r] for r in range(3)) + (
            consts[7] - (16 * served + 8).astype(F32)
        )
        scales, _q, _norm, _inverse, turned = rotation_of(values)
        scaled = [[turned[r][k] * scales[k] for k in range(3)] for r in range(3)]
        conic_a, conic_b, conic_c = conic_of(consts, scaled)
        colours = [
            0.5 + sum(consts[8 + k] * values[11 + 3 * k + c] for k in range(16)) for c in range(3)
        ]
        log_opacity = jnp.broadcast_to(log_sigmoid(values[10]), (8, 128))
        rows = [screen_u, screen_v, conic_a, conic_b, conic_c, log_opacity] + colours
        for f in range(9):
            feat_out[i, f] = rows[f]
        return carry

    lax.fori_loop(0, 4, serve, 0)


def three(x):
    high = x.astype(BF16).astype(F32)
    rest = x - high
    middle = rest.astype(BF16).astype(F32)
    return high, middle, rest - middle


def dot_nn(a, b):
    return lax.dot_general(a, b, (((1,), (0,)), ((), ())), preferred_element_type=F32)


def dot_nt(a, b):
    return lax.dot_general(a, b, (((1,), (1,)), ((), ())), preferred_element_type=F32)


def dot_tn(a, b):
    return lax.dot_general(a, b, (((0,), (0,)), ((), ())), preferred_element_type=F32)


CHUNK = 512


def composite(
    table_ref, list_ref, target_ref, basis_ref, basis_t_ref, rendered_out,
    onehot, feats, alpha, weight, weight_h, weight_m, colour_rows, image, grad_chunk, slot_acc,
):
    steps = CHUNK // 8
    chunks = 4096 // CHUNK
    table = table_ref[...].reshape(144, 256)
    table3 = jnp.concatenate(three(table), axis=0).astype(BF16)
    tile_of = lax.broadcasted_iota(jnp.int32, (1, CHUNK), 1) & 7
    in_tile = lax.broadcasted_iota(jnp.int32, (8, CHUNK), 0) == tile_of
    low_iota = lax.broadcasted_iota(jnp.int32, (256, CHUNK), 0)
    high_iota = lax.broadcasted_iota(jnp.int32, (16, CHUNK), 0)
    zeros_row = jnp.zeros((1, CHUNK), F32)
    image[...] = jnp.zeros_like(image)
    slot_acc[...] = jnp.zeros_like(slot_acc)

    def forward(k, through):
        cols = pl.ds(pl.multiple_of(k * CHUNK, CHUNK), CHUNK)
        index = list_ref[:, cols]
        hot = jnp.where(low_iota == (index & 255), 1.0, 0.0).astype(BF16)
        onehot[:, cols] = hot
        picked = dot_nn(table3, hot)
        picked = picked[0:144] + picked[144:288] + picked[288:432]
        here = high_iota == (index >> 8)
        rows = [
            jnp.sum(jnp.where(here, picked[f * 16:(f + 1) * 16], 0.0), axis=0, keepdims=True)
            for f in range(9)
        ]
        u = rows[0] - (16 * tile_of + 8).astype(F32)
        v, a, b, c, log_opacity = rows[1:6]
        feats[0:1, cols] = u
        feats[1:2, cols] = v
        feats[2:3, cols] = a
        feats[3:4, cols] = b
        feats[4:5, cols] = c
        live = index >= 0
        along_u = a * u + b * v
        along_v = b * u + c * v
        constant = jnp.where(live, log_opacity - 0.5 * (along_u * u + along_v * v), -16384.0)
        terms = [constant, along_u, along_v, -0.5 * a, -b, -0.5 * c]
        terms = [t * LOG2E for t in terms] + [zeros_row, zeros_row]
        terms = jnp.concatenate(terms, axis=0)
        high, middle, low = three(terms)
        terms = jnp.concatenate([high, middle, low, jnp.zeros_like(low)], axis=0).astype(BF16)
        power = dot_tn(terms, basis_ref[...])
        seen = jnp.minimum(jnp.exp2(power), 0.99)
        alpha[cols, :] = seen
        for j in range(steps):
            one = seen[8 * j:8 * j + 8]
            part = through * one
            weight[pl.ds(pl.multiple_of(k * CHUNK + 8 * j, 8), 8), :] = part
            through = through - part
        part = weight[cols, :]
        part_h = part.astype(BF16)
        part_m = (part - part_h.astype(F32)).astype(BF16)
        weight_h[cols, :] = part_h
        weight_m[cols, :] = part_m
        masked = jnp.concatenate(
            [jnp.where(in_tile, rows[6 + ch], 0.0) for ch in range(3)], axis=0
        )
        high, middle, low = three(masked)
        stacked = jnp.concatenate([high, middle, low, high, middle, high], axis=0).astype(BF16)
        colour_rows[:, cols] = stacked
        image[...] += dot_nn(stacked[0:80], part_h) + dot_nn(stacked[0:80], part_m)
        return through

    lax.fori_loop(0, chunks, forward, jnp.ones((8, 256), F32))
    picture = image[0:24] + image[24:48] + image[48:72]
    rendered_out[...] = picture
    wrong = picture - target_ref[...]
    high, middle, low = three(wrong)
    wrong_q = jnp.concatenate([high, high, high, middle, middle, low], axis=0).astype(BF16)
    wrong_w = jnp.concatenate([high, middle], axis=0).astype(BF16)

    def backward(step, behind):
        k = chunks - 1 - step
        cols = pl.ds(pl.multiple_of(k * CHUNK, CHUNK), CHUNK)
        value = dot_tn(colour_rows[:, cols], wrong_q)
        for j in reversed(range(steps)):
            at = pl.ds(pl.multiple_of(k * CHUNK + 8 * j, 8), 8)
            seen = alpha[at, :]
            gain = value[8 * j:8 * j + 8] - behind
            grad_chunk[8 * j:8 * j + 8, :] = jnp.where(seen < 0.99, weight[at, :] * gain, 0.0)
            behind = behind + seen * gain
        grad = grad_chunk[...]
        high, middle, low = three(grad)
        basis_t = basis_t_ref[...]
        moments = (
            dot_nt(basis_t, high.astype(BF16))
            + dot_nt(basis_t, middle.astype(BF16))
            + dot_nt(basis_t, low.astype(BF16))
        )
        tinted = dot_nt(wrong_w, weight_h[cols, :]) + dot_nt(wrong_w, weight_m[cols, :])
        tinted = tinted[0:24] + tinted[24:48]
        colour = [
            jnp.sum(jnp.where(in_tile, tinted[8 * ch:8 * ch + 8], 0.0), axis=0, keepdims=True)
            for ch in range(3)
        ]
        u, v, a, b, c = [feats[f:f + 1, cols] for f in range(5)]
        m1, mx, my, mxx, mxy, myy = [moments[f:f + 1] for f in range(6)]
        dx = mx - u * m1
        dy = my - v * m1
        found = [
            a * dx + b * dy,
            b * dx + c * dy,
            -0.5 * (mxx - u * (mx + dx)),
            -(mxy - u * my - v * dx),
            -0.5 * (myy - v * (my + dy)),
            m1,
        ] + colour
        found = jnp.concatenate(found + [zeros_row] * 7, axis=0)
        index = list_ref[:, cols]
        here = high_iota == (index >> 8)
        spread = [
            jnp.where(here, part[f:f + 1], 0.0) for part in three(found) for f in range(9)
        ]
        spread = jnp.concatenate(spread, axis=0).astype(BF16)
        slot_acc[...] += dot_nt(spread, onehot[:, cols])
        return behind

    lax.fori_loop(0, chunks, backward, jnp.zeros((8, 256), F32))
    total = slot_acc[0:144] + slot_acc[144:288] + slot_acc[288:432]
    return total


def window_kernel(
    feat_ref, params_ref, consts_ref, ids_ref, list_ref, target_ref, basis_ref, basis_t_ref,
    rendered_out, all_out,
    came, by_server, table, onehot, feats, alpha, weight, weight_h, weight_m, colour_rows, image,
    grad_chunk, slot_acc, to_server, back, got, gathered,
    out_send, out_recv, in_send, in_recv, back_send, back_recv, own_send, own_recv,
    far_send, far_recv, near_send, near_recv, loc_sem,
):
    cell, view, z, y, x, core = place()
    greet()

    def feature_out(i):
        source, target = feat_ref.at[i], came.at[i]
        return Or_local(
            i, view,
            lambda: remote(
                source, target, out_send.at[i], out_recv.at[i],
                requester(i, z, y, x, core), view,
            ),
            lambda: pltpu.make_async_copy(source, target, out_recv.at[i]),
        )

    def feature_in(step):
        who = (view + step) & 7
        return remote(
            came.at[:, :, who, :], by_server.at[view], in_send.at[step], in_recv.at[step], cell, who
        )

    for i in range(4):
        feature_out(i).start()
    for i in range(4):
        feature_out(i).wait_recv()
    for step in range(1, 8):
        feature_in(step).start()
    mine = pltpu.make_async_copy(came.at[:, :, view, :], by_server.at[view], loc_sem.at[0])
    mine.start()
    for i in range(4):
        feature_out(i).wait_send()
    mine.wait()
    for step in range(1, 8):
        feature_in(step).wait_recv()
    for step in range(1, 8):
        feature_in(step).wait_send()
    for who in range(8):
        for i in range(4):
            row, lanes = 2 * who + i // 2, slice((i % 2) * 128, (i % 2) * 128 + 128)
            for f in range(9):
                table[f, row:row + 1, lanes] = by_server[who, i, f:f + 1]

    total = composite(
        table, list_ref, target_ref, basis_ref, basis_t_ref, rendered_out,
        onehot, feats, alpha, weight, weight_h, weight_m, colour_rows, image, grad_chunk, slot_acc,
    )

    slot_acc[0:144] = total
    for who in range(8):
        for i in range(4):
            row, lanes = 2 * who + i // 2, slice((i % 2) * 128, (i % 2) * 128 + 128)
            for f in range(9):
                to_server[who, i, f:f + 1] = slot_acc[16 * f + row:16 * f + row + 1, lanes]

    def grad_back(step):
        who = (view + step) & 7
        return remote(
            to_server.at[who], back.at[:, :, view, :], back_send.at[step], back_recv.at[step],
            cell, who,
        )

    def grad_own(i):
        source, target = back.at[i], got.at[i]
        return Or_local(
            i, view,
            lambda: remote(
                source, target, own_send.at[i], own_recv.at[i], server(i, z, y, x, core), view
            ),
            lambda: pltpu.make_async_copy(source, target, own_recv.at[i]),
        )

    for step in range(1, 8):
        grad_back(step).start()
    mine = pltpu.make_async_copy(to_server.at[view], back.at[:, :, view, :], loc_sem.at[1])
    mine.start()
    mine.wait()
    for step in range(1, 8):
        grad_back(step).wait_recv()
    for i in range(4):
        grad_own(i).start()
    consts = [jnp.broadcast_to(consts_ref[:, k:k + 1], (8, 128)) for k in range(8)]
    for i in range(4):
        grad_own(i).wait_recv()
        values = [params_ref[i, k:k + 1] for k in range(11)]
        scales, (qw, qx, qy, qz), norm, inverse, turned = rotation_of(values)
        scaled = [[turned[r][k] * scales[k] for k in range(3)] for r in range(3)]
        a, b, c = conic_of(consts, scaled)
        du, dv, da, db, dc, dlog, d0, d1, d2 = [got[i, f] for f in range(9)]
        down = lambda t: jnp.sum(t, axis=0, keepdims=True)
        position = [down(consts[r] * du + consts[4 + r] * dv) for r in range(3)]
        half = 0.5 * db
        p00 = a * da + b * half
        p01 = a * half + b * dc
        p10 = b * da + c * half
        p11 = b * half + c * dc
        s00 = -(p00 * a + p01 * b)
        s01 = -(p00 * b + p01 * c)
        s11 = -(p10 * b + p11 * c)
        cov = {}
        for r in range(3):
            first = consts[r] * s00 + consts[4 + r] * s01
            second = consts[r] * s01 + consts[4 + r] * s11
            for t in range(r, 3):
                cov[r, t] = down(first * consts[t] + second * consts[4 + t])
                cov[t, r] = cov[r, t]
        dscaled = [
            [2.0 * sum(cov[r, t] * scaled[t][k] for t in range(3)) for k in range(3)]
            for r in range(3)
        ]
        dlogs = [sum(dscaled[r][k] * scaled[r][k] for r in range(3)) for k in range(3)]
        (e00, e01, e02), (e10, e11, e12), (e20, e21, e22) = [
            [dscaled[r][k] * scales[k] for k in range(3)] for r in range(3)
        ]
        qd = [
            2.0 * (qz * (e10 - e01) + qy * (e02 - e20) + qx * (e21 - e12)),
            2.0 * (qy * (e01 + e10) + qz * (e02 + e20) + qw * (e21 - e12) - 2.0 * qx * (e11 + e22)),
            2.0 * (qx * (e01 + e10) + qw * (e02 - e20) + qz * (e12 + e21) - 2.0 * qy * (e00 + e22)),
            2.0 * (qw * (e10 - e01) + qx * (e02 + e20) + qy * (e12 + e21) - 2.0 * qz * (e00 + e11)),
        ]
        inward = jnp.where(norm > 0.5, qw * qd[0] + qx * qd[1] + qy * qd[2] + qz * qd[3], 0.0)
        dq = [(g - q * inward) * inverse for g, q in zip(qd, (qw, qx, qy, qz))]
        dlogit = down(dlog) * (1.0 / (1.0 + jnp.exp(values[10])))
        name = ids_ref[i:i + 1].astype(F32)
        zero = jnp.zeros_like(name)
        rows = position + dlogs + dq + [dlogit, name] + [zero] * 4
        cols = pl.ds(i * 128, 128)
        gathered[view, 0:16, cols] = jnp.concatenate(rows, axis=0)
        gathered[view, 16:24, cols] = d0
        gathered[view, 24:32, cols] = d1
        gathered[view, 32:40, cols] = d2


    def far(step):
        who = (view + 2 * step) & 7
        return remote(
            gathered.at[view], gathered.at[view], far_send.at[step], far_recv.at[step], cell, who
        )

    def near(step):
        which = (view - 2 * step) & 7
        return remote(
            gathered.at[which], gathered.at[which], near_send.at[step], near_recv.at[step],
            cell, view ^ 1,
        )

    for step in (2, 1, 3):
        far(step).start()
    near(0).start()
    for step in (1, 3, 2):
        which = (view - 2 * step) & 7
        pltpu.make_async_copy(gathered.at[view], gathered.at[which], far_recv.at[step]).wait()
        near(step).start()
    for step in range(4):
        which = ((view ^ 1) - 2 * step) & 7
        pltpu.make_async_copy(gathered.at[view], gathered.at[which], near_recv.at[step]).wait()
    for step in range(1, 8):
        grad_back(step).wait_send()
    for i in range(4):
        grad_own(i).wait_send()
    for step in (1, 2, 3):
        far(step).wait_send()
    for step in range(4):
        near(step).wait_send()
    all_out[...] = gathered[...]


def place_kernel(base_ref, all_ref, mix_ref, out_ref, acc):
    base = base_ref[0]
    low_iota = lax.broadcasted_iota(jnp.int32, (256, 512), 0)
    acc[...] = jnp.zeros_like(acc)

    def one(source, carry):
        block = all_ref[source]
        name = block[11:12].astype(jnp.int32) - base
        hot = jnp.where(low_iota == (name & 255), 1.0, 0.0).astype(BF16)
        high = name >> 8
        parts = jnp.concatenate(three(block), axis=0)
        spread = jnp.concatenate(
            [
                jnp.concatenate(
                    [jnp.where(high == h, parts, 0.0), jnp.where(high == h + 1, parts, 0.0)], axis=0
                ).astype(BF16)
                for h in range(0, 16, 2)
            ],
            axis=0,
        )
        acc[...] += dot_nt(spread, hot)
        return carry

    lax.fori_loop(0, 8, one, 0)
    mix = mix_ref[...]
    for h in range(16):
        at = 120 * h
        found = acc[at:at + 40] + acc[at + 40:at + 80] + acc[at + 80:at + 120]
        out_ref[:, h * 256:(h + 1) * 256] = jnp.dot(
            mix, found, precision=lax.Precision.HIGHEST, preferred_element_type=F32
        )


def pixel_basis():
    pixel = np.arange(256)
    x = pixel % 16 - 7.5
    y = pixel // 16 - 7.5
    eight = np.stack([np.ones(256), x, y, x * x, x * y, y * y, 0 * x, 0 * x])
    wide = np.concatenate([eight, eight, eight, 0 * eight]).astype(np.float32)
    tall = np.concatenate([eight, 0 * eight]).astype(np.float32)
    return jnp.asarray(wide, BF16), jnp.asarray(tall, BF16)


VM = pl.BlockSpec(memory_space=pltpu.VMEM)
SM = pl.BlockSpec(memory_space=pltpu.SMEM)
MIB = 1024 * 1024
DMA = pltpu.SemaphoreType.DMA


def shape(*dims, dtype=F32):
    return jax.ShapeDtypeStruct(dims, dtype)


def ask(camera, ids):
    return pl.pallas_call(
        ask_kernel,
        out_shape=(shape(4, 128, dtype=jnp.int32), shape(8, 128)),
        in_specs=[VM, VM],
        out_specs=(VM, VM),
        scratch_shapes=[
            pltpu.VMEM((1, 128), F32),
            pltpu.VMEM((8, 128), F32),
            pltpu.VMEM((4, 128), jnp.int32),
            DMA, DMA((4,)), DMA((4,)), DMA((8,)), DMA((8,)),
        ],
        compiler_params=pltpu.CompilerParams(
            collective_id=0, has_side_effects=True, vmem_limit_bytes=2 * MIB
        ),
        name="ask",
    )(camera, ids)


def project(ids, cams, gaussians):
    return pl.pallas_call(
        project_kernel,
        out_shape=(shape(4, 9, 8, 128), shape(4, 16, 128), shape(8, 128)),
        in_specs=[SM, VM, pl.BlockSpec(memory_space=pl.ANY)],
        out_specs=(VM, VM, VM),
        scratch_shapes=[pltpu.VMEM((59, 32768), F32), pltpu.VMEM((64, 128), F32), DMA],
        compiler_params=pltpu.CompilerParams(vmem_limit_bytes=16 * MIB),
        name="project",
    )(ids, cams, gaussians)


def window(feat, params, consts, ids, listed, target):
    wide, tall = pixel_basis()
    return pl.pallas_call(
        window_kernel,
        out_shape=(shape(24, 256), shape(8, 40, 512)),
        in_specs=[VM] * 8,
        out_specs=(VM, VM),
        scratch_shapes=[
            pltpu.VMEM((4, 9, 8, 128), F32),
            pltpu.VMEM((8, 4, 9, 128), F32),
            pltpu.VMEM((9, 16, 256), F32),
            pltpu.VMEM((256, 4096), BF16),
            pltpu.VMEM((8, 4096), F32),
            pltpu.VMEM((4096, 256), F32),
            pltpu.VMEM((4096, 256), F32),
            pltpu.VMEM((4096, 256), BF16),
            pltpu.VMEM((4096, 256), BF16),
            pltpu.VMEM((144, 4096), BF16),
            pltpu.VMEM((80, 256), F32),
            pltpu.VMEM((CHUNK, 256), F32),
            pltpu.VMEM((432, 256), F32),
            pltpu.VMEM((8, 4, 9, 128), F32),
            pltpu.VMEM((4, 9, 8, 128), F32),
            pltpu.VMEM((4, 9, 8, 128), F32),
            pltpu.VMEM((8, 40, 512), F32),
            DMA((4,)), DMA((4,)), DMA((8,)), DMA((8,)), DMA((8,)), DMA((8,)), DMA((4,)), DMA((4,)),
            DMA((4,)), DMA((4,)), DMA((4,)), DMA((4,)), DMA((2,)),
        ],
        compiler_params=pltpu.CompilerParams(
            collective_id=1, has_side_effects=True, vmem_limit_bytes=48 * MIB
        ),
        name="window",
    )(feat, params, consts, ids, listed, target, wide, tall)


def put(base, everything, mix):
    return pl.pallas_call(
        place_kernel,
        out_shape=shape(59, 4096),
        in_specs=[SM, VM, VM],
        out_specs=VM,
        scratch_shapes=[pltpu.VMEM((1920, 256), F32)],
        compiler_params=pltpu.CompilerParams(vmem_limit_bytes=32 * MIB),
        name="put",
    )(base, everything, mix)


def mixing(consts):
    harmonics = consts[:, 8:24].T
    spread = harmonics[:, None, None, :] * jnp.eye(3, dtype=F32)[None, :, :, None]
    colour = jnp.pad(spread.reshape(48, 24), ((11, 0), (16, 0)))
    return colour + jnp.asarray(np.eye(59, 40) * (np.arange(59) < 11)[:, None], F32)


def slots_of(entries):
    _cell, _view, z, y, _x, _core = place()
    owner = entries >> 7
    dz = (z - (owner >> 2)) & 7
    dy = (y - (owner & 3)) & 3
    who = (((dy + dz) & 3) << 1) | (dz & 1)
    return (((who << 2) | (dz >> 1)) << 7) | (entries & 127)


def on_device(gaussians, cameras, fetch_ids, tile_lists, lengths, target_image):
    live = jnp.arange(512, dtype=jnp.int32)[:, None] < lengths[None, :]
    listed = jnp.where(live, slots_of(tile_lists[0]).T, -1).reshape(1, 4096)
    target = target_image.reshape(24, 256)
    ids, cams = ask(cameras, fetch_ids[0])
    feat, params, consts = project(ids, cams, gaussians)
    picture, everything = window(feat, params, consts, ids, listed, target)
    base = (lax.axis_index("view") * 4096).astype(jnp.int32).reshape(1)
    param_grads = put(base, everything, mixing(consts))
    return picture.reshape(3, 1, 8, 256), param_grads


def solution(mesh):
    in_specs = (
        P(None, "cell"),
        P("view", None),
        P("cell", None, None),
        P("view", "cell", None),
        P("cell"),
        P(None, "view", "cell", None),
    )
    out_specs = (P(None, "view", "cell", None), P(None, ("cell", "view")))
    return jax.shard_map(
        on_device, mesh=mesh, in_specs=in_specs, out_specs=out_specs, check_vma=False
    )
```

```python
import functools

import jax
import jax.numpy as jnp
import numpy as np
from jax import lax
from jax.experimental import pallas as pl
from jax.experimental.pallas import tpu as pltpu
from jax.sharding import PartitionSpec as P

MESH = pl.DeviceIdType.MESH
LOG2E = 1.4426950408889634
F32 = jnp.float32
BF16 = jnp.bfloat16

harmonic_zero = 0.28209479177387814
harmonic_one = 0.4886025119029199
harmonic_two = (
    1.0925484305920792,
    -1.0925484305920792,
    0.31539156525252005,
    -1.0925484305920792,
    0.5462742152960396,
)
harmonic_three = (
    -0.5900435899266435,
    2.890611442640554,
    -0.4570457994644658,
    0.3731763325901154,
    -0.4570457994644658,
    1.445305721320277,
    -0.5900435899266435,
)


def harmonic_basis(direction):
    along_x, along_y, along_z = (direction[0], direction[1], direction[2])
    square_x, square_y, square_z = (along_x * along_x, along_y * along_y, along_z * along_z)
    return [
        harmonic_zero + 0.0 * along_x,
        -harmonic_one * along_y,
        harmonic_one * along_z,
        -harmonic_one * along_x,
        harmonic_two[0] * along_x * along_y,
        harmonic_two[1] * along_y * along_z,
        harmonic_two[2] * (2.0 * square_z - square_x - square_y),
        harmonic_two[3] * along_x * along_z,
        harmonic_two[4] * (square_x - square_y),
        harmonic_three[0] * along_y * (3.0 * square_x - square_y),
        harmonic_three[1] * along_x * along_y * along_z,
        harmonic_three[2] * along_y * (4.0 * square_z - square_x - square_y),
        harmonic_three[3] * along_z * (2.0 * square_z - 3.0 * square_x - 3.0 * square_y),
        harmonic_three[4] * along_x * (4.0 * square_z - square_x - square_y),
        harmonic_three[5] * along_z * (square_x - square_y),
        harmonic_three[6] * along_x * (square_x - 3.0 * square_y),
    ]


def camera_columns(cams):
    cosine, sine = jnp.cos(cams), jnp.sin(cams)
    wide = lambda t, k: jnp.broadcast_to(t[:, k:k + 1], (8, 128))
    cos_yaw, cos_pitch, cos_roll = [wide(cosine, k) for k in range(3)]
    sin_yaw, sin_pitch, sin_roll = [wide(sine, k) for k in range(3)]
    shift_u, shift_v, scale_u, scale_v = [wide(cams, k) for k in range(3, 7)]
    first = [
        cos_yaw * cos_pitch,
        cos_yaw * sin_pitch * sin_roll - sin_yaw * cos_roll,
        cos_yaw * sin_pitch * cos_roll + sin_yaw * sin_roll,
    ]
    second = [
        sin_yaw * cos_pitch,
        sin_yaw * sin_pitch * sin_roll + cos_yaw * cos_roll,
        sin_yaw * sin_pitch * cos_roll - cos_yaw * sin_roll,
    ]
    third = [-sin_pitch, cos_pitch * sin_roll, cos_pitch * cos_roll]
    return (
        [scale_u * t for t in first] + [64.0 + shift_u]
        + [scale_v * t for t in second] + [256.0 + shift_v]
        + harmonic_basis(third)
    )


def place():
    cell, view = lax.axis_index("cell"), lax.axis_index("view")
    return cell, view, cell >> 2, cell & 3, view >> 1, view & 1


def requester(i, z, y, x, core):
    dz = core + 2 * i
    return (((z + dz) & 7) << 2) | ((y + x - dz) & 3)


def server(i, z, y, x, core):
    dz = core + 2 * i
    return (((z - dz) & 7) << 2) | ((y - x + dz) & 3)


def greet(meanwhile=None):
    cell, view, z, y, x, core = place()
    barrier = pltpu.get_barrier_semaphore()

    def signal(where, who):
        pl.semaphore_signal(barrier, inc=1, device_id=(where, who), device_id_type=MESH)

    for i in range(4):
        if i == 0:
            @pl.when(view != 0)
            def _():
                signal(requester(0, z, y, x, core), view)
                signal(server(0, z, y, x, core), view)
        else:
            signal(requester(i, z, y, x, core), view)
            signal(server(i, z, y, x, core), view)
    for step in range(1, 8):
        signal(cell, (view + step) & 7)
    if meanwhile is not None:
        meanwhile()
    pl.semaphore_wait(barrier, jnp.where(view == 0, 13, 15))


class Or_local:
    def __init__(self, i, view, remote, local):
        self.first, self.view, self.remote, self.local = i == 0, view, remote, local

    def each(self, remote_act, local_act):
        if not self.first:
            remote_act(self.remote())
            return

        if local_act is not None:
            @pl.when(self.view == 0)
            def _():
                local_act(self.local())

        @pl.when(self.view != 0)
        def _():
            remote_act(self.remote())

    def start(self):
        self.each(lambda c: c.start(), lambda c: c.start())

    def wait_recv(self):
        self.each(lambda c: c.wait_recv(), lambda c: c.wait())

    def wait_send(self):
        self.each(lambda c: c.wait_send(), None)


def remote(source, target, send, recv, where, who):
    return pltpu.make_async_remote_copy(
        src_ref=source, dst_ref=target, send_sem=send, recv_sem=recv,
        device_id=(where, who), device_id_type=MESH,
    )


def rotation_of(values):
    scales = [jnp.exp(values[3 + k]) for k in range(3)]
    norm = jnp.sqrt(
        values[6] * values[6] + values[7] * values[7] + values[8] * values[8] + values[9] * values[9]
    )
    inverse = 1.0 / jnp.maximum(norm, 0.5)
    qw, qx, qy, qz = [values[6 + k] * inverse for k in range(4)]
    turned = [
        [1.0 - 2.0 * (qy * qy + qz * qz), 2.0 * (qx * qy - qw * qz), 2.0 * (qx * qz + qw * qy)],
        [2.0 * (qx * qy + qw * qz), 1.0 - 2.0 * (qx * qx + qz * qz), 2.0 * (qy * qz - qw * qx)],
        [2.0 * (qx * qz - qw * qy), 2.0 * (qy * qz + qw * qx), 1.0 - 2.0 * (qx * qx + qy * qy)],
    ]
    return scales, (qw, qx, qy, qz), norm, inverse, turned


PAIRS = ((0, 0), (0, 1), (0, 2), (1, 1), (1, 2), (2, 2))


def symmetric(rows):
    full = dict(zip(PAIRS, rows))
    return [[full[min(r, t), max(r, t)] for t in range(3)] for r in range(3)]


def conic_of(consts, cov):
    first = [sum(consts[r] * cov[r][t] for r in range(3)) for t in range(3)]
    second = [sum(consts[4 + r] * cov[r][t] for r in range(3)) for t in range(3)]
    uu = sum(first[t] * consts[t] for t in range(3)) + 0.3
    uv = sum(first[t] * consts[4 + t] for t in range(3))
    vv = sum(second[t] * consts[4 + t] for t in range(3)) + 0.3
    inverse = 1.0 / (uu * vv - uv * uv)
    return vv * inverse, -uv * inverse, uu * inverse


def log_sigmoid(x):
    return jnp.minimum(x, 0.0) - jnp.log(1.0 + jnp.exp(-jnp.abs(x)))


def ask_kernel(
    cam_ref, fetch_ref, gauss_ref, ids_out, cams_out, tab_out,
    tab_sem, row, cams, idv, loc_sem, id_send, id_recv, cam_send, cam_recv,
):
    cell, view, z, y, x, core = place()
    whole = pltpu.make_async_copy(gauss_ref, tab_out, tab_sem)
    whole.start()
    row[...] = jnp.zeros_like(row)
    row[:, 0:7] = cam_ref[...]
    greet()

    def id_copy(i):
        owner = server(i, z, y, x, core)
        source, target = fetch_ref.at[pl.ds(owner, 1)], idv.at[pl.ds(i, 1)]
        return Or_local(
            i, view,
            lambda: remote(source, target, id_send.at[i], id_recv.at[i], owner, view),
            lambda: pltpu.make_async_copy(source, target, id_recv.at[i]),
        )

    def cam_copy(step):
        return remote(
            row, cams.at[pl.ds(view, 1)], cam_send.at[step], cam_recv.at[step],
            cell, (view + step) & 7,
        )

    for i in range(4):
        id_copy(i).start()
    for step in range(1, 8):
        cam_copy(step).start()
    mine = pltpu.make_async_copy(row, cams.at[pl.ds(view, 1)], loc_sem)
    mine.start()
    for i in range(4):
        id_copy(i).wait_recv()
    ids_out[...] = idv[...]
    for step in range(1, 8):
        cam_copy(step).wait_recv()
    mine.wait()
    cams_out[...] = cams[...]
    for i in range(4):
        id_copy(i).wait_send()
    for step in range(1, 8):
        cam_copy(step).wait_send()
    whole.wait()


def project_kernel(ids_ref, cams_ref, tab, brief_out, params_out, consts_out, mix_out, got):
    consts = camera_columns(cams_ref[...])
    lanes = lax.broadcasted_iota(jnp.int32, (8, 128), 1)
    packed = jnp.zeros((8, 128), F32)
    for k in range(8):
        packed = jnp.where(lanes == k, consts[k], packed)
    consts_out[...] = packed
    rows16 = lax.broadcasted_iota(jnp.int32, (16, 128), 0)
    lanes16 = lax.broadcasted_iota(jnp.int32, (16, 128), 1)
    mix_out[0:16] = jnp.where((rows16 == lanes16) & (rows16 < 11), 1.0, 0.0)
    for c in range(3):
        part = jnp.zeros((8, 128), F32)
        for k in range(16):
            part = jnp.where(lanes == 11 + 3 * k + c, consts[8 + k], part)
        mix_out[16 + 8 * c:24 + 8 * c] = part
    lane = lax.broadcasted_iota(jnp.int32, (59, 128), 1)

    def serve(i, carry):
        acc = jnp.zeros((59, 128), F32)
        for n in range(128):
            name = ids_ref[i, n]
            block = tab[:, pl.ds(pl.multiple_of((name >> 7) << 7, 128), 128)]
            acc = jnp.where(lane == n, pltpu.roll(block, (n - name) & 127, 1), acc)
        got[0:59] = acc
        params_out[i] = got[0:16]
        values = [got[k:k + 1] for k in range(59)]
        scales, _q, _norm, _inverse, turned = rotation_of(values)
        scaled = [[turned[r][k] * scales[k] for k in range(3)] for r in range(3)]
        cov = [sum(scaled[r][k] * scaled[t][k] for k in range(3)) for r, t in PAIRS]
        rows = values[0:3] + cov + [log_sigmoid(values[10])] + [jnp.zeros((1, 128), F32)] * 6
        brief_out[i, 0:16] = jnp.concatenate(rows, axis=0)
        for c in range(3):
            brief_out[i, 16 + 8 * c:24 + 8 * c] = 0.5 + sum(
                consts[8 + k] * values[11 + 3 * k + c] for k in range(16)
            )
        return carry

    lax.fori_loop(0, 4, serve, 0)


def three(x):
    high = x.astype(BF16).astype(F32)
    rest = x - high
    middle = rest.astype(BF16).astype(F32)
    return high, middle, rest - middle


def dot_nn(a, b):
    return lax.dot_general(a, b, (((1,), (0,)), ((), ())), preferred_element_type=F32)


def dot_nt(a, b):
    return lax.dot_general(a, b, (((1,), (1,)), ((), ())), preferred_element_type=F32)


def dot_tn(a, b):
    return lax.dot_general(a, b, (((0,), (0,)), ((), ())), preferred_element_type=F32)


CHUNK = 1024


def mark(list_ref, onehot):
    low_iota = lax.broadcasted_iota(jnp.int32, (256, 256), 0)

    def one(k, carry):
        cols = pl.ds(pl.multiple_of(k * 256, 256), 256)
        onehot[:, cols] = jnp.where(low_iota == (list_ref[:, cols] & 255), 1.0, 0.0).astype(BF16)
        return carry

    lax.fori_loop(0, 16, one, 0)


def composite(
    table_ref, list_ref, target_ref, basis_ref, basis_t_ref, rendered_out,
    onehot, feats, alpha, weight, weight_h, weight_m, colour_rows, image, grad_chunk, slot_acc,
):
    steps = CHUNK // 8
    chunks = 4096 // CHUNK
    table = table_ref[...].reshape(144, 256)
    table3 = jnp.concatenate(three(table), axis=0).astype(BF16)
    tile_of = lax.broadcasted_iota(jnp.int32, (1, CHUNK), 1) & 7
    in_tile = lax.broadcasted_iota(jnp.int32, (8, CHUNK), 0) == tile_of
    high_iota = lax.broadcasted_iota(jnp.int32, (16, CHUNK), 0)
    zeros_row = jnp.zeros((1, CHUNK), F32)
    image[...] = jnp.zeros_like(image)
    slot_acc[...] = jnp.zeros_like(slot_acc)

    def forward(k, through):
        cols = pl.ds(pl.multiple_of(k * CHUNK, CHUNK), CHUNK)
        index = list_ref[:, cols]
        picked = dot_nn(table3, onehot[:, cols])
        picked = picked[0:144] + picked[144:288] + picked[288:432]
        here = high_iota == (index >> 8)
        rows = [
            jnp.sum(jnp.where(here, picked[f * 16:(f + 1) * 16], 0.0), axis=0, keepdims=True)
            for f in range(9)
        ]
        u = rows[0] - (16 * tile_of + 8).astype(F32)
        v, a, b, c, log_opacity = rows[1:6]
        feats[0:1, cols] = u
        feats[1:2, cols] = v
        feats[2:3, cols] = a
        feats[3:4, cols] = b
        feats[4:5, cols] = c
        live = index >= 0
        along_u = a * u + b * v
        along_v = b * u + c * v
        constant = jnp.where(live, log_opacity - 0.5 * (along_u * u + along_v * v), -16384.0)
        terms = [constant, along_u, along_v, -0.5 * a, -b, -0.5 * c]
        terms = [t * LOG2E for t in terms] + [zeros_row, zeros_row]
        terms = jnp.concatenate(terms, axis=0)
        high, middle, low = three(terms)
        terms = jnp.concatenate([high, middle, low, jnp.zeros_like(low)], axis=0).astype(BF16)
        power = dot_tn(terms, basis_ref[...])
        seen = jnp.minimum(jnp.exp2(power), 0.99)
        alpha[cols, :] = seen
        for j in range(steps):
            one = seen[8 * j:8 * j + 8]
            weight[pl.ds(pl.multiple_of(k * CHUNK + 8 * j, 8), 8), :] = through * one
            through = through * (1.0 - one)
        part = weight[cols, :]
        part_h = part.astype(BF16)
        part_m = (part - part_h.astype(F32)).astype(BF16)
        weight_h[cols, :] = part_h
        weight_m[cols, :] = part_m
        masked = jnp.concatenate(
            [jnp.where(in_tile, rows[6 + ch], 0.0) for ch in range(3)], axis=0
        )
        high, middle, low = three(masked)
        stacked = jnp.concatenate([high, middle, high, jnp.zeros((8, CHUNK), F32)], axis=0).astype(BF16)
        colour_rows[:, cols] = stacked
        image[...] += dot_nn(stacked[0:48], part_h) + dot_nn(stacked[0:48], part_m)
        return through

    lax.fori_loop(0, chunks, forward, jnp.ones((8, 256), F32))
    picture = image[0:24] + image[24:48]
    rendered_out[...] = picture
    wrong = picture - target_ref[...]
    high, middle, low = three(wrong)
    wrong_q = jnp.concatenate([high, high, middle, jnp.zeros((8, 256), F32)], axis=0).astype(BF16)
    wrong_w = jnp.concatenate([high, middle], axis=0).astype(BF16)

    def backward(step, behind):
        k = chunks - 1 - step
        cols = pl.ds(pl.multiple_of(k * CHUNK, CHUNK), CHUNK)
        value = dot_tn(colour_rows[:, cols], wrong_q)
        for j in reversed(range(steps)):
            at = pl.ds(pl.multiple_of(k * CHUNK + 8 * j, 8), 8)
            seen = alpha[at, :]
            gain = value[8 * j:8 * j + 8] - behind
            grad_chunk[8 * j:8 * j + 8, :] = jnp.where(seen < 0.99, weight[at, :] * gain, 0.0)
            behind = behind * (1.0 - seen) + seen * value[8 * j:8 * j + 8]
        grad = grad_chunk[...]
        high, middle, low = three(grad)
        basis_t = basis_t_ref[...]
        moments = (
            dot_nt(basis_t, high.astype(BF16))
            + dot_nt(basis_t, middle.astype(BF16))
            + dot_nt(basis_t, low.astype(BF16))
        )
        tinted = dot_nt(wrong_w, weight_h[cols, :]) + dot_nt(wrong_w, weight_m[cols, :])
        tinted = tinted[0:24] + tinted[24:48]
        colour = [
            jnp.sum(jnp.where(in_tile, tinted[8 * ch:8 * ch + 8], 0.0), axis=0, keepdims=True)
            for ch in range(3)
        ]
        u, v, a, b, c = [feats[f:f + 1, cols] for f in range(5)]
        m1, mx, my, mxx, mxy, myy = [moments[f:f + 1] for f in range(6)]
        dx = mx - u * m1
        dy = my - v * m1
        found = [
            a * dx + b * dy,
            b * dx + c * dy,
            -0.5 * (mxx - u * (mx + dx)),
            -(mxy - u * my - v * dx),
            -0.5 * (myy - v * (my + dy)),
            m1,
        ] + colour
        found = jnp.concatenate(found + [zeros_row] * 7, axis=0)
        index = list_ref[:, cols]
        here = high_iota == (index >> 8)
        spread = [
            jnp.where(here, part[f:f + 1], 0.0) for part in three(found)[:2] for f in range(9)
        ]
        spread = jnp.concatenate(spread, axis=0).astype(BF16)
        slot_acc[...] += dot_nt(spread, onehot[:, cols])
        return behind

    lax.fori_loop(0, chunks, backward, jnp.zeros((8, 256), F32))
    total = slot_acc[0:144] + slot_acc[144:288]
    return total


def window_kernel(
    brief_ref, params_ref, consts_ref, ids_ref, list_ref, target_ref, basis_ref, basis_t_ref, mix_ref,
    rendered_out, grads_out,
    came, feat, by_server, table, onehot, feats, alpha, weight, weight_h, weight_m, colour_rows,
    image, grad_chunk, slot_acc, to_server, back, sums, got, gathered, acc,
    out_send, out_recv, in_send, in_recv, back_send, back_recv, own_send, own_recv,
    far_send, far_recv, near_send, near_recv, loc_sem,
):
    cell, view, z, y, x, core = place()
    greet(lambda: mark(list_ref, onehot))
    consts = [jnp.broadcast_to(consts_ref[:, k:k + 1], (8, 128)) for k in range(8)]
    down = lambda t: jnp.sum(t, axis=0, keepdims=True)

    def brief_copy(i):
        source, target = brief_ref.at[i], came.at[i]
        return Or_local(
            i, view,
            lambda: remote(
                source, target, out_send.at[i], out_recv.at[i],
                requester(i, z, y, x, core), view,
            ),
            lambda: pltpu.make_async_copy(source, target, out_recv.at[i]),
        )

    def feature_copy(step, i):
        who = (view + step) & 7
        return remote(
            feat.at[i, :, who, :], by_server.at[view, i], in_send.at[step], in_recv.at[step],
            cell, who,
        )

    def feature_copies(step):
        who = (view + step) & 7
        return remote(
            feat.at[:, :, who, :], by_server.at[view], in_send.at[step], in_recv.at[step], cell, who
        )

    for i in (2, 1, 3, 0):
        brief_copy(i).start()
    for i in (0, 3, 1, 2):
        brief_copy(i).wait_recv()
        rows = [came[i, k:k + 1] for k in range(10)]
        feat[i, 0] = sum(consts[r] * rows[r] for r in range(3)) + consts[3]
        feat[i, 1] = sum(consts[4 + r] * rows[r] for r in range(3)) + (
            consts[7] - (16 * cell + 8).astype(F32)
        )
        for f, part in enumerate(conic_of(consts, symmetric(rows[3:9]))):
            feat[i, 2 + f] = part
        feat[i, 5] = jnp.broadcast_to(rows[9], (8, 128))
        for c in range(3):
            feat[i, 6 + c] = came[i, 16 + 8 * c:24 + 8 * c]
        for step in range(1, 8):
            feature_copy(step, i).start()
    mine = pltpu.make_async_copy(feat.at[:, :, view, :], by_server.at[view], loc_sem.at[0])
    mine.start()
    mine.wait()
    for step in range(1, 8):
        feature_copies(step).wait_recv()
    for who in range(8):
        for i in range(4):
            row, lanes = 2 * who + i // 2, slice((i % 2) * 128, (i % 2) * 128 + 128)
            for f in range(9):
                table[f, row:row + 1, lanes] = by_server[who, i, f:f + 1]

    total = composite(
        table, list_ref, target_ref, basis_ref, basis_t_ref, rendered_out,
        onehot, feats, alpha, weight, weight_h, weight_m, colour_rows, image, grad_chunk, slot_acc,
    )

    slot_acc[0:144] = total
    for who in range(8):
        for i in range(4):
            row, lanes = 2 * who + i // 2, slice((i % 2) * 128, (i % 2) * 128 + 128)
            for f in range(9):
                to_server[who, i, f:f + 1] = slot_acc[16 * f + row:16 * f + row + 1, lanes]

    def grad_back(step):
        who = (view + step) & 7
        return remote(
            to_server.at[who], back.at[:, :, view, :], back_send.at[step], back_recv.at[step],
            cell, who,
        )

    def sum_copy(i):
        source, target = sums.at[i], got.at[i]
        return Or_local(
            i, view,
            lambda: remote(
                source, target, own_send.at[i], own_recv.at[i], server(i, z, y, x, core), view
            ),
            lambda: pltpu.make_async_copy(source, target, own_recv.at[i]),
        )

    for step in range(1, 8):
        grad_back(step).start()
    mine = pltpu.make_async_copy(to_server.at[view], back.at[:, :, view, :], loc_sem.at[1])
    mine.start()
    acc[...] = jnp.zeros_like(acc)
    mine.wait()
    for step in range(1, 8):
        grad_back(step).wait_recv()
    zero = jnp.zeros((1, 128), F32)
    for i in (2, 1, 3, 0):
        a, b, c = [feat[i, f] for f in range(2, 5)]
        du, dv, da, db, dc, dlog = [back[i, f] for f in range(6)]
        position = [down(consts[r] * du + consts[4 + r] * dv) for r in range(3)]
        half = 0.5 * db
        p00 = a * da + b * half
        p01 = a * half + b * dc
        p10 = b * da + c * half
        p11 = b * half + c * dc
        s00 = -(p00 * a + p01 * b)
        s01 = -(p00 * b + p01 * c)
        s11 = -(p10 * b + p11 * c)
        first = [consts[r] * s00 + consts[4 + r] * s01 for r in range(3)]
        second = [consts[r] * s01 + consts[4 + r] * s11 for r in range(3)]
        cov = [down(first[r] * consts[t] + second[r] * consts[4 + t]) for r, t in PAIRS]
        sums[i, 0:16] = jnp.concatenate(position + cov + [down(dlog)] + [zero] * 6, axis=0)
        for c in range(3):
            sums[i, 16 + 8 * c:24 + 8 * c] = back[i, 6 + c]
        sum_copy(i).start()
    for i in (0, 3, 1, 2):
        sum_copy(i).wait_recv()
        values = [params_ref[i, k:k + 1] for k in range(11)]
        scales, (qw, qx, qy, qz), norm, inverse, turned = rotation_of(values)
        scaled = [[turned[r][k] * scales[k] for k in range(3)] for r in range(3)]
        cov = symmetric([got[i, 3 + k:4 + k] for k in range(6)])
        dscaled = [
            [2.0 * sum(cov[r][t] * scaled[t][k] for t in range(3)) for k in range(3)]
            for r in range(3)
        ]
        dlogs = [sum(dscaled[r][k] * scaled[r][k] for r in range(3)) for k in range(3)]
        (e00, e01, e02), (e10, e11, e12), (e20, e21, e22) = [
            [dscaled[r][k] * scales[k] for k in range(3)] for r in range(3)
        ]
        qd = [
            2.0 * (qz * (e10 - e01) + qy * (e02 - e20) + qx * (e21 - e12)),
            2.0 * (qy * (e01 + e10) + qz * (e02 + e20) + qw * (e21 - e12) - 2.0 * qx * (e11 + e22)),
            2.0 * (qx * (e01 + e10) + qw * (e02 - e20) + qz * (e12 + e21) - 2.0 * qy * (e00 + e22)),
            2.0 * (qw * (e10 - e01) + qx * (e02 + e20) + qy * (e12 + e21) - 2.0 * qz * (e00 + e11)),
        ]
        inward = jnp.where(norm > 0.5, qw * qd[0] + qx * qd[1] + qy * qd[2] + qz * qd[3], 0.0)
        dq = [(g - q * inward) * inverse for g, q in zip(qd, (qw, qx, qy, qz))]
        dlogit = got[i, 9:10] * (1.0 / (1.0 + jnp.exp(values[10])))
        name = ids_ref[i:i + 1].astype(F32)
        position = [got[i, k:k + 1] for k in range(3)]
        rows = position + dlogs + dq + [dlogit, name] + [zero] * 4
        cols = pl.ds(i * 128, 128)
        gathered[view, 0:16, cols] = jnp.concatenate(rows, axis=0)
        gathered[view, 16:40, cols] = got[i, 16:40]

    def far(step):
        who = (view + 2 * step) & 7
        return remote(
            gathered.at[view], gathered.at[view], far_send.at[step], far_recv.at[step], cell, who
        )

    def near(step):
        which = (view - 2 * step) & 7
        return remote(
            gathered.at[which], gathered.at[which], near_send.at[step], near_recv.at[step],
            cell, view ^ 1,
        )

    def far_came(step):
        which = (view - 2 * step) & 7
        pltpu.make_async_copy(gathered.at[view], gathered.at[which], far_recv.at[step]).wait()
        near(step).start()
        return which

    def near_came(step):
        which = ((view ^ 1) - 2 * step) & 7
        pltpu.make_async_copy(gathered.at[view], gathered.at[which], near_recv.at[step]).wait()
        return which

    base = (view * 4096).astype(F32)
    low_iota = lax.broadcasted_iota(jnp.int32, (256, 512), 0)

    def deposit(which):
        block = gathered[which]
        name = (block[11:12] - base).astype(jnp.int32)
        hot = jnp.where(low_iota == (name & 255), 1.0, 0.0).astype(BF16)
        row = name >> 8
        parts = jnp.concatenate(three(block)[:2], axis=0)
        spread = [jnp.where(row == h, parts, 0.0).astype(BF16) for h in range(16)]
        acc[...] += dot_nt(jnp.concatenate(spread, axis=0), hot)

    for step in (2, 1, 3):
        far(step).start()
    near(0).start()
    deposit(view)
    deposit(near_came(0))
    one, three_ = far_came(1), far_came(3)
    deposit(one)
    two = far_came(2)
    deposit(three_)
    deposit(two)
    for step in (1, 3, 2):
        deposit(near_came(step))

    mix = mix_ref[...].T[0:59]
    for h in range(16):
        at = 80 * h
        grads_out[:, h * 256:(h + 1) * 256] = jnp.dot(
            mix, acc[at:at + 40] + acc[at + 40:at + 80],
            precision=lax.Precision.HIGHEST, preferred_element_type=F32,
        )
    for i in range(4):
        brief_copy(i).wait_send()
    for step in range(1, 8):
        feature_copies(step).wait_send()
    for step in range(1, 8):
        grad_back(step).wait_send()
    for i in range(4):
        sum_copy(i).wait_send()
    for step in (1, 2, 3):
        far(step).wait_send()
    for step in range(4):
        near(step).wait_send()


def pixel_basis():
    pixel = np.arange(256)
    x = pixel % 16 - 7.5
    y = pixel // 16 - 7.5
    eight = np.stack([np.ones(256), x, y, x * x, x * y, y * y, 0 * x, 0 * x])
    wide = np.concatenate([eight, eight, eight, 0 * eight]).astype(np.float32)
    tall = np.concatenate([eight, 0 * eight]).astype(np.float32)
    return jnp.asarray(wide, BF16), jnp.asarray(tall, BF16)


VM = pl.BlockSpec(memory_space=pltpu.VMEM)
SM = pl.BlockSpec(memory_space=pltpu.SMEM)
MIB = 1024 * 1024
DMA = pltpu.SemaphoreType.DMA


def shape(*dims, dtype=F32):
    return jax.ShapeDtypeStruct(dims, dtype)


def ask(camera, ids, gaussians):
    return pl.pallas_call(
        ask_kernel,
        out_shape=(shape(4, 128, dtype=jnp.int32), shape(8, 128), shape(59, 32768)),
        in_specs=[VM, VM, pl.BlockSpec(memory_space=pltpu.HBM)],
        out_specs=(VM, VM, pl.BlockSpec(memory_space=pl.ANY)),
        scratch_shapes=[
            DMA,
            pltpu.VMEM((1, 128), F32),
            pltpu.VMEM((8, 128), F32),
            pltpu.VMEM((4, 128), jnp.int32),
            DMA, DMA((4,)), DMA((4,)), DMA((8,)), DMA((8,)),
        ],
        compiler_params=pltpu.CompilerParams(
            collective_id=0, has_side_effects=True, vmem_limit_bytes=44 * MIB
        ),
        name="ask",
    )(camera, ids, gaussians)


def project(ids, cams, gaussians):
    return pl.pallas_call(
        project_kernel,
        out_shape=(shape(4, 40, 128), shape(4, 16, 128), shape(8, 128), shape(40, 128)),
        in_specs=[SM, VM, VM],
        out_specs=(VM, VM, VM, VM),
        scratch_shapes=[pltpu.VMEM((64, 128), F32)],
        compiler_params=pltpu.CompilerParams(vmem_limit_bytes=16 * MIB),
        name="project",
    )(ids, cams, gaussians)


def window(brief, params, consts, ids, listed, target, mix):
    wide, tall = pixel_basis()
    return pl.pallas_call(
        window_kernel,
        out_shape=(shape(24, 256), shape(59, 4096)),
        in_specs=[VM] * 9,
        out_specs=(VM, VM),
        scratch_shapes=[
            pltpu.VMEM((4, 40, 128), F32),
            pltpu.VMEM((4, 9, 8, 128), F32),
            pltpu.VMEM((8, 4, 9, 128), F32),
            pltpu.VMEM((9, 16, 256), F32),
            pltpu.VMEM((256, 4096), BF16),
            pltpu.VMEM((8, 4096), F32),
            pltpu.VMEM((4096, 256), F32),
            pltpu.VMEM((4096, 256), F32),
            pltpu.VMEM((4096, 256), BF16),
            pltpu.VMEM((4096, 256), BF16),
            pltpu.VMEM((80, 4096), BF16),
            pltpu.VMEM((48, 256), F32),
            pltpu.VMEM((CHUNK, 256), F32),
            pltpu.VMEM((288, 256), F32),
            pltpu.VMEM((8, 4, 9, 128), F32),
            pltpu.VMEM((4, 9, 8, 128), F32),
            pltpu.VMEM((4, 40, 128), F32),
            pltpu.VMEM((4, 40, 128), F32),
            pltpu.VMEM((8, 40, 512), F32),
            pltpu.VMEM((1280, 256), F32),
            DMA((4,)), DMA((4,)), DMA((8,)), DMA((8,)), DMA((8,)), DMA((8,)), DMA((4,)), DMA((4,)),
            DMA((4,)), DMA((4,)), DMA((4,)), DMA((4,)), DMA((2,)),
        ],
        compiler_params=pltpu.CompilerParams(
            collective_id=1, has_side_effects=True, vmem_limit_bytes=48 * MIB
        ),
        name="window",
    )(brief, params, consts, ids, listed, target, wide, tall, mix)


def slots_of(entries):
    _cell, _view, z, y, _x, _core = place()
    owner = entries >> 7
    dz = (z - (owner >> 2)) & 7
    dy = (y - (owner & 3)) & 3
    who = (((dy + dz) & 3) << 1) | (dz & 1)
    return (((who << 2) | (dz >> 1)) << 7) | (entries & 127)


def on_device(gaussians, cameras, fetch_ids, tile_lists, lengths, target_image):
    live = jnp.arange(512, dtype=jnp.int32)[:, None] < lengths[None, :]
    listed = jnp.where(live, slots_of(tile_lists[0]).T, -1).reshape(1, 4096)
    target = target_image.reshape(24, 256)
    ids, cams, table = ask(cameras, fetch_ids[0], gaussians)
    brief, params, consts, mix = project(ids, cams, table)
    picture, param_grads = window(brief, params, consts, ids, listed, target, mix)
    return picture.reshape(3, 1, 8, 256), param_grads


def solution(mesh):
    in_specs = (
        P(None, "cell"),
        P("view", None),
        P("cell", None, None),
        P("view", "cell", None),
        P("cell"),
        P(None, "view", "cell", None),
    )
    out_specs = (P(None, "view", "cell", None), P(None, ("cell", "view")))
    return jax.shard_map(
        on_device, mesh=mesh, in_specs=in_specs, out_specs=out_specs, check_vma=False
    )
```

```python
import functools

import jax
import jax.numpy as jnp
import numpy as np
from jax import lax
from jax.experimental import pallas as pl
from jax.experimental.pallas import tpu as pltpu
from jax.sharding import PartitionSpec as P

MESH = pl.DeviceIdType.MESH
LOG2E = 1.4426950408889634
F32 = jnp.float32
BF16 = jnp.bfloat16

harmonic_zero = 0.28209479177387814
harmonic_one = 0.4886025119029199
harmonic_two = (
    1.0925484305920792,
    -1.0925484305920792,
    0.31539156525252005,
    -1.0925484305920792,
    0.5462742152960396,
)
harmonic_three = (
    -0.5900435899266435,
    2.890611442640554,
    -0.4570457994644658,
    0.3731763325901154,
    -0.4570457994644658,
    1.445305721320277,
    -0.5900435899266435,
)


def harmonic_basis(direction):
    along_x, along_y, along_z = (direction[0], direction[1], direction[2])
    square_x, square_y, square_z = (along_x * along_x, along_y * along_y, along_z * along_z)
    return [
        harmonic_zero + 0.0 * along_x,
        -harmonic_one * along_y,
        harmonic_one * along_z,
        -harmonic_one * along_x,
        harmonic_two[0] * along_x * along_y,
        harmonic_two[1] * along_y * along_z,
        harmonic_two[2] * (2.0 * square_z - square_x - square_y),
        harmonic_two[3] * along_x * along_z,
        harmonic_two[4] * (square_x - square_y),
        harmonic_three[0] * along_y * (3.0 * square_x - square_y),
        harmonic_three[1] * along_x * along_y * along_z,
        harmonic_three[2] * along_y * (4.0 * square_z - square_x - square_y),
        harmonic_three[3] * along_z * (2.0 * square_z - 3.0 * square_x - 3.0 * square_y),
        harmonic_three[4] * along_x * (4.0 * square_z - square_x - square_y),
        harmonic_three[5] * along_z * (square_x - square_y),
        harmonic_three[6] * along_x * (square_x - 3.0 * square_y),
    ]


def camera_columns(cams):
    cosine, sine = jnp.cos(cams), jnp.sin(cams)
    wide = lambda t, k: jnp.broadcast_to(t[:, k:k + 1], (8, 128))
    cos_yaw, cos_pitch, cos_roll = [wide(cosine, k) for k in range(3)]
    sin_yaw, sin_pitch, sin_roll = [wide(sine, k) for k in range(3)]
    shift_u, shift_v, scale_u, scale_v = [wide(cams, k) for k in range(3, 7)]
    first = [
        cos_yaw * cos_pitch,
        cos_yaw * sin_pitch * sin_roll - sin_yaw * cos_roll,
        cos_yaw * sin_pitch * cos_roll + sin_yaw * sin_roll,
    ]
    second = [
        sin_yaw * cos_pitch,
        sin_yaw * sin_pitch * sin_roll + cos_yaw * cos_roll,
        sin_yaw * sin_pitch * cos_roll - cos_yaw * sin_roll,
    ]
    third = [-sin_pitch, cos_pitch * sin_roll, cos_pitch * cos_roll]
    return (
        [scale_u * t for t in first] + [64.0 + shift_u]
        + [scale_v * t for t in second] + [256.0 + shift_v]
        + harmonic_basis(third)
    )


def place():
    cell, view = lax.axis_index("cell"), lax.axis_index("view")
    return cell, view, cell >> 2, cell & 3, view >> 1, view & 1


def requester(i, z, y, x, core):
    dz = core + 2 * i
    return (((z + dz) & 7) << 2) | ((y + x - dz) & 3)


def server(i, z, y, x, core):
    dz = core + 2 * i
    return (((z - dz) & 7) << 2) | ((y - x + dz) & 3)


def hello(where, who):
    pl.semaphore_signal(
        pltpu.get_barrier_semaphore(), inc=1, device_id=(where, who), device_id_type=MESH
    )


def greet_ask():
    cell, view, z, y, x, core = place()
    for i in range(4):
        if i == 0:
            @pl.when(view != 0)
            def _():
                hello(requester(0, z, y, x, core), view)
        else:
            hello(requester(i, z, y, x, core), view)
    for step in range(1, 8):
        hello(cell, (view + step) & 7)
    pl.semaphore_wait(pltpu.get_barrier_semaphore(), jnp.where(view == 0, 10, 11))


OFFSETS = [(dz, dy) for dz in (4, 3, 5, 2, 6, 1, 7, 0) for dy in (2, 1, 3, 0)]


def owner_at(offset, z, y):
    dz, dy = offset
    return (((z - dz) & 7) << 2) | ((y - dy) & 3), (((dy + dz) & 3) << 1) | (dz & 1), dz >> 1


def greet_window(meanwhile):
    cell, view, z, y, x, core = place()
    for offset in OFFSETS:
        owner, who, _i = owner_at(offset, z, y)
        if offset == (0, 0):
            @pl.when(view != 0)
            def _():
                hello(owner, who)
        else:
            hello(owner, who)
    for step in range(1, 4):
        hello(cell, (view + 2 * step) & 7)
    hello(cell, view ^ 1)
    meanwhile()
    pl.semaphore_wait(pltpu.get_barrier_semaphore(), jnp.where(view == 0, 35, 36))


def slot_window(ref, owner):
    return ref.at[:, owner >> 1, pl.ds(pl.multiple_of((owner & 1) * 128, 128), 128)]


class Or_local:
    def __init__(self, i, view, remote, local):
        self.first, self.view, self.remote, self.local = i == 0, view, remote, local

    def each(self, remote_act, local_act):
        if not self.first:
            remote_act(self.remote())
            return

        if local_act is not None:
            @pl.when(self.view == 0)
            def _():
                local_act(self.local())

        @pl.when(self.view != 0)
        def _():
            remote_act(self.remote())

    def start(self):
        self.each(lambda c: c.start(), lambda c: c.start())

    def wait_recv(self):
        self.each(lambda c: c.wait_recv(), lambda c: c.wait())

    def wait_send(self):
        self.each(lambda c: c.wait_send(), None)


def remote(source, target, send, recv, where, who):
    return pltpu.make_async_remote_copy(
        src_ref=source, dst_ref=target, send_sem=send, recv_sem=recv,
        device_id=(where, who), device_id_type=MESH,
    )


def rotation_of(values):
    scales = [jnp.exp(values[3 + k]) for k in range(3)]
    norm = jnp.sqrt(
        values[6] * values[6] + values[7] * values[7] + values[8] * values[8] + values[9] * values[9]
    )
    inverse = 1.0 / jnp.maximum(norm, 0.5)
    qw, qx, qy, qz = [values[6 + k] * inverse for k in range(4)]
    turned = [
        [1.0 - 2.0 * (qy * qy + qz * qz), 2.0 * (qx * qy - qw * qz), 2.0 * (qx * qz + qw * qy)],
        [2.0 * (qx * qy + qw * qz), 1.0 - 2.0 * (qx * qx + qz * qz), 2.0 * (qy * qz - qw * qx)],
        [2.0 * (qx * qz - qw * qy), 2.0 * (qy * qz + qw * qx), 1.0 - 2.0 * (qx * qx + qy * qy)],
    ]
    return scales, (qw, qx, qy, qz), norm, inverse, turned


PAIRS = ((0, 0), (0, 1), (0, 2), (1, 1), (1, 2), (2, 2))


def symmetric(rows):
    full = dict(zip(PAIRS, rows))
    return [[full[min(r, t), max(r, t)] for t in range(3)] for r in range(3)]


def conic_of(consts, cov):
    first = [sum(consts[r] * cov[r][t] for r in range(3)) for t in range(3)]
    second = [sum(consts[4 + r] * cov[r][t] for r in range(3)) for t in range(3)]
    uu = sum(first[t] * consts[t] for t in range(3)) + 0.3
    uv = sum(first[t] * consts[4 + t] for t in range(3))
    vv = sum(second[t] * consts[4 + t] for t in range(3)) + 0.3
    inverse = 1.0 / (uu * vv - uv * uv)
    return vv * inverse, -uv * inverse, uu * inverse


def log_sigmoid(x):
    return jnp.minimum(x, 0.0) - jnp.log(1.0 + jnp.exp(-jnp.abs(x)))


def ask_kernel(
    cam_ref, fetch_ref, gauss_ref, ids_out, cams_out, tab_out,
    tab_sem, row, cams, idv, loc_sem, id_send, id_recv, cam_send, cam_recv,
):
    cell, view, z, y, x, core = place()
    whole = pltpu.make_async_copy(gauss_ref, tab_out, tab_sem)
    whole.start()
    row[...] = jnp.zeros_like(row)
    row[:, 0:7] = cam_ref[...]
    greet_ask()

    def id_copy(i):
        owner = server(i, z, y, x, core)
        source, target = fetch_ref.at[pl.ds(owner, 1)], idv.at[pl.ds(i, 1)]
        return Or_local(
            i, view,
            lambda: remote(source, target, id_send.at[i], id_recv.at[i], owner, view),
            lambda: pltpu.make_async_copy(source, target, id_recv.at[i]),
        )

    def cam_copy(step):
        return remote(
            row, cams.at[pl.ds(view, 1)], cam_send.at[step], cam_recv.at[step],
            cell, (view + step) & 7,
        )

    for i in range(4):
        id_copy(i).start()
    for step in range(1, 8):
        cam_copy(step).start()
    mine = pltpu.make_async_copy(row, cams.at[pl.ds(view, 1)], loc_sem)
    mine.start()
    for i in range(4):
        id_copy(i).wait_recv()
    ids_out[...] = idv[...]
    for step in range(1, 8):
        cam_copy(step).wait_recv()
    mine.wait()
    cams_out[...] = cams[...]
    for i in range(4):
        id_copy(i).wait_send()
    for step in range(1, 8):
        cam_copy(step).wait_send()
    whole.wait()


def project_kernel(ids_ref, cams_ref, tab, feat_out, params_out, consts_out, mix_out, got):
    cell, view, z, y, x, core = place()
    consts = camera_columns(cams_ref[...])
    lanes = lax.broadcasted_iota(jnp.int32, (8, 128), 1)
    packed = jnp.zeros((8, 128), F32)
    for k in range(8):
        packed = jnp.where(lanes == k, consts[k], packed)
    consts_out[...] = packed
    rows16 = lax.broadcasted_iota(jnp.int32, (16, 128), 0)
    lanes16 = lax.broadcasted_iota(jnp.int32, (16, 128), 1)
    mix_out[0:16] = jnp.where((rows16 == lanes16) & (rows16 < 11), 1.0, 0.0)
    for c in range(3):
        part = jnp.zeros((8, 128), F32)
        for k in range(16):
            part = jnp.where(lanes == 11 + 3 * k + c, consts[8 + k], part)
        mix_out[16 + 8 * c:24 + 8 * c] = part
    lane = lax.broadcasted_iota(jnp.int32, (59, 128), 1)

    def serve(i, carry):
        acc = jnp.zeros((59, 128), F32)
        for n in range(128):
            name = ids_ref[i, n]
            block = tab[:, pl.ds(pl.multiple_of((name >> 7) << 7, 128), 128)]
            acc = jnp.where(lane == n, pltpu.roll(block, (n - name) & 127, 1), acc)
        got[0:59] = acc
        params_out[i] = got[0:16]
        values = [got[k:k + 1] for k in range(59)]
        scales, _q, _norm, _inverse, turned = rotation_of(values)
        scaled = [[turned[r][k] * scales[k] for k in range(3)] for r in range(3)]
        cov = [sum(scaled[r][k] * scaled[t][k] for k in range(3)) for r, t in PAIRS]
        served = requester(i, z, y, x, core)
        feat_out[i, 0] = sum(consts[r] * values[r] for r in range(3)) + consts[3]
        feat_out[i, 1] = sum(consts[4 + r] * values[r] for r in range(3)) + (
            consts[7] - (16 * served + 8).astype(F32)
        )
        for f, part in enumerate(conic_of(consts, symmetric(cov))):
            feat_out[i, 2 + f] = part
        feat_out[i, 5] = jnp.broadcast_to(log_sigmoid(values[10]), (8, 128))
        for c in range(3):
            feat_out[i, 6 + c] = 0.5 + sum(
                consts[8 + k] * values[11 + 3 * k + c] for k in range(16)
            )
        return carry

    lax.fori_loop(0, 4, serve, 0)


def three(x):
    high = x.astype(BF16).astype(F32)
    rest = x - high
    middle = rest.astype(BF16).astype(F32)
    return high, middle, rest - middle


def dot_nn(a, b):
    return lax.dot_general(a, b, (((1,), (0,)), ((), ())), preferred_element_type=F32)


def dot_nt(a, b):
    return lax.dot_general(a, b, (((1,), (1,)), ((), ())), preferred_element_type=F32)


def dot_tn(a, b):
    return lax.dot_general(a, b, (((0,), (0,)), ((), ())), preferred_element_type=F32)


CHUNK = 2048


def mark(list_ref, onehot):
    low_iota = lax.broadcasted_iota(jnp.int32, (256, 256), 0)

    def one(k, carry):
        cols = pl.ds(pl.multiple_of(k * 256, 256), 256)
        onehot[:, cols] = jnp.where(low_iota == (list_ref[:, cols] & 255), 1.0, 0.0).astype(BF16)
        return carry

    lax.fori_loop(0, 16, one, 0)


def composite(
    table_ref, list_ref, target_ref, basis_ref, basis_t_ref, rendered_out,
    onehot, feats, alpha, weight, weight_h, weight_m, colour_rows, image, grad_chunk, slot_acc,
):
    steps = CHUNK // 8
    chunks = 4096 // CHUNK
    table = table_ref[...].reshape(144, 256)
    table3 = jnp.concatenate(three(table), axis=0).astype(BF16)
    tile_of = lax.broadcasted_iota(jnp.int32, (1, CHUNK), 1) & 7
    in_tile = lax.broadcasted_iota(jnp.int32, (8, CHUNK), 0) == tile_of
    high_iota = lax.broadcasted_iota(jnp.int32, (16, CHUNK), 0)
    zeros_row = jnp.zeros((1, CHUNK), F32)
    image[...] = jnp.zeros_like(image)
    slot_acc[...] = jnp.zeros_like(slot_acc)

    def forward(k, through):
        cols = pl.ds(pl.multiple_of(k * CHUNK, CHUNK), CHUNK)
        index = list_ref[:, cols]
        picked = dot_nn(table3, onehot[:, cols])
        picked = picked[0:144] + picked[144:288] + picked[288:432]
        here = high_iota == (index >> 8)
        rows = [
            jnp.sum(jnp.where(here, picked[f * 16:(f + 1) * 16], 0.0), axis=0, keepdims=True)
            for f in range(9)
        ]
        u = rows[0] - (16 * tile_of + 8).astype(F32)
        v, a, b, c, log_opacity = rows[1:6]
        feats[0:1, cols] = u
        feats[1:2, cols] = v
        feats[2:3, cols] = a
        feats[3:4, cols] = b
        feats[4:5, cols] = c
        live = index >= 0
        along_u = a * u + b * v
        along_v = b * u + c * v
        constant = jnp.where(live, log_opacity - 0.5 * (along_u * u + along_v * v), -16384.0)
        terms = [constant, along_u, along_v, -0.5 * a, -b, -0.5 * c]
        terms = [t * LOG2E for t in terms] + [zeros_row, zeros_row]
        terms = jnp.concatenate(terms, axis=0)
        high, middle, low = three(terms)
        terms = jnp.concatenate([high, middle, low, jnp.zeros_like(low)], axis=0).astype(BF16)
        power = dot_tn(terms, basis_ref[...])
        seen = jnp.minimum(jnp.exp2(power), 0.99)
        alpha[cols, :] = seen
        for j in range(steps):
            one = seen[8 * j:8 * j + 8]
            weight[pl.ds(pl.multiple_of(k * CHUNK + 8 * j, 8), 8), :] = through * one
            through = through * (1.0 - one)
        part = weight[cols, :]
        part_h = part.astype(BF16)
        part_m = (part - part_h.astype(F32)).astype(BF16)
        weight_h[cols, :] = part_h
        weight_m[cols, :] = part_m
        masked = jnp.concatenate(
            [jnp.where(in_tile, rows[6 + ch], 0.0) for ch in range(3)], axis=0
        )
        high, middle, low = three(masked)
        stacked = jnp.concatenate([high, middle, high, jnp.zeros((8, CHUNK), F32)], axis=0).astype(BF16)
        colour_rows[:, cols] = stacked
        image[...] += dot_nn(stacked[0:48], part_h) + dot_nn(stacked[0:48], part_m)
        return through

    lax.fori_loop(0, chunks, forward, jnp.ones((8, 256), F32))
    picture = image[0:24] + image[24:48]
    rendered_out[...] = picture
    wrong = picture - target_ref[...]
    high, middle, low = three(wrong)
    wrong_q = jnp.concatenate([high, high, middle, jnp.zeros((8, 256), F32)], axis=0).astype(BF16)
    wrong_w = jnp.concatenate([high, middle], axis=0).astype(BF16)

    def backward(step, behind):
        k = chunks - 1 - step
        cols = pl.ds(pl.multiple_of(k * CHUNK, CHUNK), CHUNK)
        value = dot_tn(colour_rows[:, cols], wrong_q)
        for j in reversed(range(steps)):
            at = pl.ds(pl.multiple_of(k * CHUNK + 8 * j, 8), 8)
            seen = alpha[at, :]
            gain = value[8 * j:8 * j + 8] - behind
            grad_chunk[8 * j:8 * j + 8, :] = jnp.where(seen < 0.99, weight[at, :] * gain, 0.0)
            behind = behind * (1.0 - seen) + seen * value[8 * j:8 * j + 8]
        grad = grad_chunk[...]
        high, middle, low = three(grad)
        basis_t = basis_t_ref[...]
        moments = (
            dot_nt(basis_t, high.astype(BF16))
            + dot_nt(basis_t, middle.astype(BF16))
            + dot_nt(basis_t, low.astype(BF16))
        )
        tinted = dot_nt(wrong_w, weight_h[cols, :]) + dot_nt(wrong_w, weight_m[cols, :])
        tinted = tinted[0:24] + tinted[24:48]
        colour = [
            jnp.sum(jnp.where(in_tile, tinted[8 * ch:8 * ch + 8], 0.0), axis=0, keepdims=True)
            for ch in range(3)
        ]
        u, v, a, b, c = [feats[f:f + 1, cols] for f in range(5)]
        m1, mx, my, mxx, mxy, myy = [moments[f:f + 1] for f in range(6)]
        dx = mx - u * m1
        dy = my - v * m1
        found = [
            a * dx + b * dy,
            b * dx + c * dy,
            -0.5 * (mxx - u * (mx + dx)),
            -(mxy - u * my - v * dx),
            -0.5 * (myy - v * (my + dy)),
            m1,
        ] + colour
        found = jnp.concatenate(found + [zeros_row] * 7, axis=0)
        index = list_ref[:, cols]
        here = high_iota == (index >> 8)
        spread = [
            jnp.where(here, part[f:f + 1], 0.0) for part in three(found)[:2] for f in range(9)
        ]
        spread = jnp.concatenate(spread, axis=0).astype(BF16)
        slot_acc[...] += dot_nt(spread, onehot[:, cols])
        return behind

    lax.fori_loop(0, chunks, backward, jnp.zeros((8, 256), F32))
    total = slot_acc[0:144] + slot_acc[144:288]
    return total


def window_kernel(
    feat_ref, params_ref, consts_ref, ids_ref, list_ref, target_ref, basis_ref, basis_t_ref, mix_ref,
    rendered_out, grads_out,
    table, onehot, feats, alpha, weight, weight_h, weight_m, colour_rows,
    image, grad_chunk, slot_acc, leaving, got, gathered, acc,
    f_send, f_recv, b_send, b_recv, far_send, far_recv, near_send, near_recv,
):
    cell, view, z, y, x, core = place()
    greet_window(lambda: mark(list_ref, onehot))
    consts = [jnp.broadcast_to(consts_ref[:, k:k + 1], (8, 128)) for k in range(8)]
    down = lambda t: jnp.sum(t, axis=0, keepdims=True)

    def feature_copy(i, v):
        source, target = feat_ref.at[i, :, v, :], slot_window(table, cell)
        return Or_local(
            i + v, view,
            lambda: remote(
                source, target, f_send.at[i * 8 + v], f_recv.at[cell],
                requester(i, z, y, x, core), v,
            ),
            lambda: pltpu.make_async_copy(source, target, f_recv.at[cell]),
        )

    for i in (2, 1, 3, 0):
        for v in range(8):
            feature_copy(i, v).start()

    def arrived(owner, carry):
        pltpu.make_async_copy(
            feat_ref.at[0, :, 0, :], slot_window(table, owner), f_recv.at[owner]
        ).wait()
        return carry

    lax.fori_loop(0, 32, arrived, 0)

    total = composite(
        table, list_ref, target_ref, basis_ref, basis_t_ref, rendered_out,
        onehot, feats, alpha, weight, weight_h, weight_m, colour_rows, image, grad_chunk, slot_acc,
    )
    leaving[...] = total.reshape(9, 16, 256)

    def grad_copy(n):
        owner, who, i = owner_at(OFFSETS[n], z, y)
        source, target = slot_window(leaving, owner), got.at[i, :, view, :]
        return Or_local(
            31 - n, view,
            lambda: remote(source, target, b_send.at[n], b_recv.at[i * 8 + view], owner, who),
            lambda: pltpu.make_async_copy(source, target, b_recv.at[i * 8 + view]),
        )

    for n in range(32):
        grad_copy(n).start()
    acc[...] = jnp.zeros_like(acc)

    def far(step, i):
        who = (view + 2 * step) & 7
        return remote(
            gathered.at[view, i], gathered.at[view, i], far_send.at[step, i], far_recv.at[step, i],
            cell, who,
        )

    def near(step, i):
        which = (view - 2 * step) & 7
        return remote(
            gathered.at[which, i], gathered.at[which, i],
            near_send.at[step, i], near_recv.at[step, i], cell, view ^ 1,
        )

    values = [
        jnp.concatenate([params_ref[i, k:k + 1] for i in range(4)], axis=1) for k in range(11)
    ]
    all_scales, all_turns, all_norm, all_inverse, turned = rotation_of(values)
    all_scaled = [turned[r][k] * all_scales[k] for r in range(3) for k in range(3)]
    all_faint = 1.0 / (1.0 + jnp.exp(values[10]))
    zero = jnp.zeros((1, 128), F32)
    order = (0, 3, 1, 2)
    for i in order:
        for v in range(8):
            pltpu.make_async_copy(
                slot_window(leaving, cell), got.at[i, :, v, :], b_recv.at[i * 8 + v]
            ).wait()
        a, b, c = [feat_ref[i, f] for f in range(2, 5)]
        du, dv, da, db, dc, dlog = [got[i, f] for f in range(6)]
        position = [down(consts[r] * du + consts[4 + r] * dv) for r in range(3)]
        half = 0.5 * db
        p00 = a * da + b * half
        p01 = a * half + b * dc
        p10 = b * da + c * half
        p11 = b * half + c * dc
        s00 = -(p00 * a + p01 * b)
        s01 = -(p00 * b + p01 * c)
        s11 = -(p10 * b + p11 * c)
        first = [consts[r] * s00 + consts[4 + r] * s01 for r in range(3)]
        second = [consts[r] * s01 + consts[4 + r] * s11 for r in range(3)]
        cov = [down(first[r] * consts[t] + second[r] * consts[4 + t]) for r, t in PAIRS]
        lanes = slice(128 * i, 128 * i + 128)
        scales, (qw, qx, qy, qz), scaled = [
            [t[:, lanes] for t in group] for group in (all_scales, all_turns, all_scaled)
        ]
        scaled = [scaled[3 * r:3 * r + 3] for r in range(3)]
        inverse, faint = all_inverse[:, lanes], all_faint[:, lanes]
        cov = symmetric(cov)
        dscaled = [
            [2.0 * sum(cov[r][t] * scaled[t][k] for t in range(3)) for k in range(3)]
            for r in range(3)
        ]
        dlogs = [sum(dscaled[r][k] * scaled[r][k] for r in range(3)) for k in range(3)]
        (e00, e01, e02), (e10, e11, e12), (e20, e21, e22) = [
            [dscaled[r][k] * scales[k] for k in range(3)] for r in range(3)
        ]
        qd = [
            2.0 * (qz * (e10 - e01) + qy * (e02 - e20) + qx * (e21 - e12)),
            2.0 * (qy * (e01 + e10) + qz * (e02 + e20) + qw * (e21 - e12) - 2.0 * qx * (e11 + e22)),
            2.0 * (qx * (e01 + e10) + qw * (e02 - e20) + qz * (e12 + e21) - 2.0 * qy * (e00 + e22)),
            2.0 * (qw * (e10 - e01) + qx * (e02 + e20) + qy * (e12 + e21) - 2.0 * qz * (e00 + e11)),
        ]
        inward = jnp.where(all_norm[:, lanes] > 0.5, qw * qd[0] + qx * qd[1] + qy * qd[2] + qz * qd[3], 0.0)
        dq = [(g - q * inward) * inverse for g, q in zip(qd, (qw, qx, qy, qz))]
        dlogit = down(dlog) * faint
        name = ids_ref[i:i + 1].astype(F32)
        rows = position + dlogs + dq + [dlogit, name] + [zero] * 4
        gathered[view, i, 0:16] = jnp.concatenate(rows, axis=0)
        for ch in range(3):
            gathered[view, i, 16 + 8 * ch:24 + 8 * ch] = got[i, 6 + ch]
        for step in (2, 1, 3):
            far(step, i).start()
        near(0, i).start()

    def far_came(step, i):
        which = (view - 2 * step) & 7
        pltpu.make_async_copy(
            gathered.at[view, i], gathered.at[which, i], far_recv.at[step, i]
        ).wait()
        near(step, i).start()

    def near_came(step):
        which = ((view ^ 1) - 2 * step) & 7
        for i in order:
            pltpu.make_async_copy(
                gathered.at[view, i], gathered.at[which, i], near_recv.at[step, i]
            ).wait()
        return which

    base = (view * 4096).astype(F32)
    low_iota = lax.broadcasted_iota(jnp.int32, (256, 512), 0)

    def deposit(which):
        block = jnp.concatenate([gathered[which, i] for i in range(4)], axis=1)
        name = (block[11:12] - base).astype(jnp.int32)
        hot = jnp.where(low_iota == (name & 255), 1.0, 0.0).astype(BF16)
        row = name >> 8
        parts = jnp.concatenate(three(block)[:2], axis=0)
        spread = [jnp.where(row == h, parts, 0.0).astype(BF16) for h in range(16)]
        acc[...] += dot_nt(jnp.concatenate(spread, axis=0), hot)

    deposit(view)
    for i in order:
        far_came(1, i)
        far_came(3, i)
    deposit(near_came(0))
    for i in order:
        far_came(2, i)
    for step in (1, 3, 2):
        deposit((view - 2 * step) & 7)
    for step in (1, 3, 2):
        deposit(near_came(step))

    mix = mix_ref[...].T[0:59]
    for h in range(16):
        at = 80 * h
        grads_out[:, h * 256:(h + 1) * 256] = jnp.dot(
            mix, acc[at:at + 40] + acc[at + 40:at + 80],
            precision=lax.Precision.HIGHEST, preferred_element_type=F32,
        )
    for i in range(4):
        for v in range(8):
            feature_copy(i, v).wait_send()
    for n in range(32):
        grad_copy(n).wait_send()
    for i in range(4):
        for step in (1, 2, 3):
            far(step, i).wait_send()
        for step in range(4):
            near(step, i).wait_send()


def pixel_basis():
    pixel = np.arange(256)
    x = pixel % 16 - 7.5
    y = pixel // 16 - 7.5
    eight = np.stack([np.ones(256), x, y, x * x, x * y, y * y, 0 * x, 0 * x])
    wide = np.concatenate([eight, eight, eight, 0 * eight]).astype(np.float32)
    tall = np.concatenate([eight, 0 * eight]).astype(np.float32)
    return jnp.asarray(wide, BF16), jnp.asarray(tall, BF16)


VM = pl.BlockSpec(memory_space=pltpu.VMEM)
SM = pl.BlockSpec(memory_space=pltpu.SMEM)
MIB = 1024 * 1024
DMA = pltpu.SemaphoreType.DMA


def shape(*dims, dtype=F32):
    return jax.ShapeDtypeStruct(dims, dtype)


def ask(camera, ids, gaussians):
    return pl.pallas_call(
        ask_kernel,
        out_shape=(shape(4, 128, dtype=jnp.int32), shape(8, 128), shape(59, 32768)),
        in_specs=[VM, VM, pl.BlockSpec(memory_space=pltpu.HBM)],
        out_specs=(VM, VM, pl.BlockSpec(memory_space=pl.ANY)),
        scratch_shapes=[
            DMA,
            pltpu.VMEM((1, 128), F32),
            pltpu.VMEM((8, 128), F32),
            pltpu.VMEM((4, 128), jnp.int32),
            DMA, DMA((4,)), DMA((4,)), DMA((8,)), DMA((8,)),
        ],
        compiler_params=pltpu.CompilerParams(
            collective_id=0, has_side_effects=True, vmem_limit_bytes=44 * MIB
        ),
        name="ask",
    )(camera, ids, gaussians)


def project(ids, cams, gaussians):
    return pl.pallas_call(
        project_kernel,
        out_shape=(shape(4, 9, 8, 128), shape(4, 16, 128), shape(8, 128), shape(40, 128)),
        in_specs=[SM, VM, VM],
        out_specs=(VM, VM, VM, VM),
        scratch_shapes=[pltpu.VMEM((64, 128), F32)],
        compiler_params=pltpu.CompilerParams(vmem_limit_bytes=16 * MIB),
        name="project",
    )(ids, cams, gaussians)


def window(feat, params, consts, ids, listed, target, mix):
    wide, tall = pixel_basis()
    return pl.pallas_call(
        window_kernel,
        out_shape=(shape(24, 256), shape(59, 4096)),
        in_specs=[VM] * 9,
        out_specs=(VM, VM),
        scratch_shapes=[
            pltpu.VMEM((9, 16, 256), F32),
            pltpu.VMEM((256, 4096), BF16),
            pltpu.VMEM((8, 4096), F32),
            pltpu.VMEM((4096, 256), F32),
            pltpu.VMEM((4096, 256), F32),
            pltpu.VMEM((4096, 256), BF16),
            pltpu.VMEM((4096, 256), BF16),
            pltpu.VMEM((80, 4096), BF16),
            pltpu.VMEM((48, 256), F32),
            pltpu.VMEM((CHUNK, 256), F32),
            pltpu.VMEM((288, 256), F32),
            pltpu.VMEM((9, 16, 256), F32),
            pltpu.VMEM((4, 9, 8, 128), F32),
            pltpu.VMEM((8, 4, 40, 128), F32),
            pltpu.VMEM((1280, 256), F32),
            DMA((32,)), DMA((32,)), DMA((32,)), DMA((32,)),
            DMA((4, 4)), DMA((4, 4)), DMA((4, 4)), DMA((4, 4)),
        ],
        compiler_params=pltpu.CompilerParams(
            collective_id=1, has_side_effects=True, vmem_limit_bytes=48 * MIB
        ),
        name="window",
    )(feat, params, consts, ids, listed, target, wide, tall, mix)


def on_device(gaussians, cameras, fetch_ids, tile_lists, lengths, target_image):
    live = jnp.arange(512, dtype=jnp.int32)[:, None] < lengths[None, :]
    listed = jnp.where(live, tile_lists[0].T, -1).reshape(1, 4096)
    target = target_image.reshape(24, 256)
    ids, cams, table = ask(cameras, fetch_ids[0], gaussians)
    feat, params, consts, mix = project(ids, cams, table)
    picture, param_grads = window(feat, params, consts, ids, listed, target, mix)
    return picture.reshape(3, 1, 8, 256), param_grads


def solution(mesh):
    in_specs = (
        P(None, "cell"),
        P("view", None),
        P("cell", None, None),
        P("view", "cell", None),
        P("cell"),
        P(None, "view", "cell", None),
    )
    out_specs = (P(None, "view", "cell", None), P(None, ("cell", "view")))
    return jax.shard_map(
        on_device, mesh=mesh, in_specs=in_specs, out_specs=out_specs, check_vma=False
    )
```

```python
import functools

import jax
import jax.numpy as jnp
import numpy as np
from jax import lax
from jax.experimental import pallas as pl
from jax.experimental.pallas import tpu as pltpu
from jax.sharding import PartitionSpec as P

MESH = pl.DeviceIdType.MESH
LOG2E = 1.4426950408889634
F32 = jnp.float32
BF16 = jnp.bfloat16

harmonic_zero = 0.28209479177387814
harmonic_one = 0.4886025119029199
harmonic_two = (
    1.0925484305920792,
    -1.0925484305920792,
    0.31539156525252005,
    -1.0925484305920792,
    0.5462742152960396,
)
harmonic_three = (
    -0.5900435899266435,
    2.890611442640554,
    -0.4570457994644658,
    0.3731763325901154,
    -0.4570457994644658,
    1.445305721320277,
    -0.5900435899266435,
)


def harmonic_basis(direction):
    along_x, along_y, along_z = (direction[0], direction[1], direction[2])
    square_x, square_y, square_z = (along_x * along_x, along_y * along_y, along_z * along_z)
    return [
        harmonic_zero + 0.0 * along_x,
        -harmonic_one * along_y,
        harmonic_one * along_z,
        -harmonic_one * along_x,
        harmonic_two[0] * along_x * along_y,
        harmonic_two[1] * along_y * along_z,
        harmonic_two[2] * (2.0 * square_z - square_x - square_y),
        harmonic_two[3] * along_x * along_z,
        harmonic_two[4] * (square_x - square_y),
        harmonic_three[0] * along_y * (3.0 * square_x - square_y),
        harmonic_three[1] * along_x * along_y * along_z,
        harmonic_three[2] * along_y * (4.0 * square_z - square_x - square_y),
        harmonic_three[3] * along_z * (2.0 * square_z - 3.0 * square_x - 3.0 * square_y),
        harmonic_three[4] * along_x * (4.0 * square_z - square_x - square_y),
        harmonic_three[5] * along_z * (square_x - square_y),
        harmonic_three[6] * along_x * (square_x - 3.0 * square_y),
    ]


def camera_columns(cams):
    cosine, sine = jnp.cos(cams), jnp.sin(cams)
    wide = lambda t, k: jnp.broadcast_to(t[:, k:k + 1], (8, 128))
    cos_yaw, cos_pitch, cos_roll = [wide(cosine, k) for k in range(3)]
    sin_yaw, sin_pitch, sin_roll = [wide(sine, k) for k in range(3)]
    shift_u, shift_v, scale_u, scale_v = [wide(cams, k) for k in range(3, 7)]
    first = [
        cos_yaw * cos_pitch,
        cos_yaw * sin_pitch * sin_roll - sin_yaw * cos_roll,
        cos_yaw * sin_pitch * cos_roll + sin_yaw * sin_roll,
    ]
    second = [
        sin_yaw * cos_pitch,
        sin_yaw * sin_pitch * sin_roll + cos_yaw * cos_roll,
        sin_yaw * sin_pitch * cos_roll - cos_yaw * sin_roll,
    ]
    third = [-sin_pitch, cos_pitch * sin_roll, cos_pitch * cos_roll]
    return (
        [scale_u * t for t in first] + [64.0 + shift_u]
        + [scale_v * t for t in second] + [256.0 + shift_v]
        + harmonic_basis(third)
    )


def place():
    cell, view = lax.axis_index("cell"), lax.axis_index("view")
    return cell, view, cell >> 2, cell & 3, view >> 1, view & 1


def requester(i, z, y, x, core):
    dz = core + 2 * i
    return (((z + dz) & 7) << 2) | ((y + x - dz) & 3)


def server(i, z, y, x, core):
    dz = core + 2 * i
    return (((z - dz) & 7) << 2) | ((y - x + dz) & 3)


def hello(where, who):
    pl.semaphore_signal(
        pltpu.get_barrier_semaphore(), inc=1, device_id=(where, who), device_id_type=MESH
    )


def greet_ask():
    cell, view, z, y, x, core = place()
    for i in range(4):
        if i == 0:
            @pl.when(view != 0)
            def _():
                hello(requester(0, z, y, x, core), view)
        else:
            hello(requester(i, z, y, x, core), view)
    for step in range(1, 8):
        hello(cell, (view + step) & 7)
    pl.semaphore_wait(pltpu.get_barrier_semaphore(), jnp.where(view == 0, 10, 11))


OFFSETS = [(dz, dy) for dz in (4, 3, 5, 2, 6, 1, 7, 0) for dy in (2, 1, 3, 0)]


def owner_at(offset, z, y):
    dz, dy = offset
    return (((z - dz) & 7) << 2) | ((y - dy) & 3), (((dy + dz) & 3) << 1) | (dz & 1), dz >> 1


def greet_window(meanwhile):
    cell, view, z, y, x, core = place()
    for offset in OFFSETS:
        owner, who, _i = owner_at(offset, z, y)
        if offset == (0, 0):
            @pl.when(view != 0)
            def _():
                hello(owner, who)
        else:
            hello(owner, who)
    for step in range(1, 4):
        hello(cell, (view + 2 * step) & 7)
    hello(cell, view ^ 1)
    meanwhile()
    pl.semaphore_wait(pltpu.get_barrier_semaphore(), jnp.where(view == 0, 35, 36))


def slot_window(ref, owner):
    return ref.at[:, owner >> 1, pl.ds(pl.multiple_of((owner & 1) * 128, 128), 128)]


class Or_local:
    def __init__(self, i, view, remote, local):
        self.first, self.view, self.remote, self.local = i == 0, view, remote, local

    def each(self, remote_act, local_act):
        if not self.first:
            remote_act(self.remote())
            return

        if local_act is not None:
            @pl.when(self.view == 0)
            def _():
                local_act(self.local())

        @pl.when(self.view != 0)
        def _():
            remote_act(self.remote())

    def start(self):
        self.each(lambda c: c.start(), lambda c: c.start())

    def wait_recv(self):
        self.each(lambda c: c.wait_recv(), lambda c: c.wait())

    def wait_send(self):
        self.each(lambda c: c.wait_send(), None)


def remote(source, target, send, recv, where, who):
    return pltpu.make_async_remote_copy(
        src_ref=source, dst_ref=target, send_sem=send, recv_sem=recv,
        device_id=(where, who), device_id_type=MESH,
    )


def rotation_of(values):
    scales = [jnp.exp(values[3 + k]) for k in range(3)]
    norm = jnp.sqrt(
        values[6] * values[6] + values[7] * values[7] + values[8] * values[8] + values[9] * values[9]
    )
    inverse = 1.0 / jnp.maximum(norm, 0.5)
    qw, qx, qy, qz = [values[6 + k] * inverse for k in range(4)]
    turned = [
        [1.0 - 2.0 * (qy * qy + qz * qz), 2.0 * (qx * qy - qw * qz), 2.0 * (qx * qz + qw * qy)],
        [2.0 * (qx * qy + qw * qz), 1.0 - 2.0 * (qx * qx + qz * qz), 2.0 * (qy * qz - qw * qx)],
        [2.0 * (qx * qz - qw * qy), 2.0 * (qy * qz + qw * qx), 1.0 - 2.0 * (qx * qx + qy * qy)],
    ]
    return scales, (qw, qx, qy, qz), norm, inverse, turned


PAIRS = ((0, 0), (0, 1), (0, 2), (1, 1), (1, 2), (2, 2))


def symmetric(rows):
    full = dict(zip(PAIRS, rows))
    return [[full[min(r, t), max(r, t)] for t in range(3)] for r in range(3)]


def conic_of(consts, cov):
    first = [sum(consts[r] * cov[r][t] for r in range(3)) for t in range(3)]
    second = [sum(consts[4 + r] * cov[r][t] for r in range(3)) for t in range(3)]
    uu = sum(first[t] * consts[t] for t in range(3)) + 0.3
    uv = sum(first[t] * consts[4 + t] for t in range(3))
    vv = sum(second[t] * consts[4 + t] for t in range(3)) + 0.3
    inverse = 1.0 / (uu * vv - uv * uv)
    return vv * inverse, -uv * inverse, uu * inverse


def log_sigmoid(x):
    return jnp.minimum(x, 0.0) - jnp.log(1.0 + jnp.exp(-jnp.abs(x)))


def ask_kernel(
    cam_ref, fetch_ref, gauss_ref, ids_out, cams_out, tab_out,
    tab_sem, row, cams, idv, loc_sem, id_send, id_recv, cam_send, cam_recv,
):
    cell, view, z, y, x, core = place()
    whole = pltpu.make_async_copy(gauss_ref, tab_out, tab_sem)
    whole.start()
    row[...] = jnp.zeros_like(row)
    row[:, 0:7] = cam_ref[...]
    greet_ask()

    def id_copy(i):
        owner = server(i, z, y, x, core)
        source, target = fetch_ref.at[pl.ds(owner, 1)], idv.at[pl.ds(i, 1)]
        return Or_local(
            i, view,
            lambda: remote(source, target, id_send.at[i], id_recv.at[i], owner, view),
            lambda: pltpu.make_async_copy(source, target, id_recv.at[i]),
        )

    def cam_copy(step):
        return remote(
            row, cams.at[pl.ds(view, 1)], cam_send.at[step], cam_recv.at[step],
            cell, (view + step) & 7,
        )

    for i in range(4):
        id_copy(i).start()
    for step in range(1, 8):
        cam_copy(step).start()
    mine = pltpu.make_async_copy(row, cams.at[pl.ds(view, 1)], loc_sem)
    mine.start()
    for i in range(4):
        id_copy(i).wait_recv()
    ids_out[...] = idv[...]
    for step in range(1, 8):
        cam_copy(step).wait_recv()
    mine.wait()
    cams_out[...] = cams[...]
    for i in range(4):
        id_copy(i).wait_send()
    for step in range(1, 8):
        cam_copy(step).wait_send()
    whole.wait()


def project_kernel(ids_ref, cams_ref, tab, feat_out, params_out, consts_out, mix_out, got):
    cell, view, z, y, x, core = place()
    consts = camera_columns(cams_ref[...])
    lanes = lax.broadcasted_iota(jnp.int32, (8, 128), 1)
    packed = jnp.zeros((8, 128), F32)
    for k in range(8):
        packed = jnp.where(lanes == k, consts[k], packed)
    consts_out[...] = packed
    rows16 = lax.broadcasted_iota(jnp.int32, (16, 128), 0)
    lanes16 = lax.broadcasted_iota(jnp.int32, (16, 128), 1)
    mix_out[0:16] = jnp.where((rows16 == lanes16) & (rows16 < 11), 1.0, 0.0)
    for c in range(3):
        part = jnp.zeros((8, 128), F32)
        for k in range(16):
            part = jnp.where(lanes == 11 + 3 * k + c, consts[8 + k], part)
        mix_out[16 + 8 * c:24 + 8 * c] = part
    lane = lax.broadcasted_iota(jnp.int32, (59, 128), 1)

    def serve(i, carry):
        acc = jnp.zeros((59, 128), F32)
        for n in range(128):
            name = ids_ref[i, n]
            block = tab[:, pl.ds(pl.multiple_of((name >> 7) << 7, 128), 128)]
            acc = jnp.where(lane == n, pltpu.roll(block, (n - name) & 127, 1), acc)
        got[0:59] = acc
        params_out[i] = got[0:16]
        values = [got[k:k + 1] for k in range(59)]
        scales, _q, _norm, _inverse, turned = rotation_of(values)
        scaled = [[turned[r][k] * scales[k] for k in range(3)] for r in range(3)]
        cov = [sum(scaled[r][k] * scaled[t][k] for k in range(3)) for r, t in PAIRS]
        served = requester(i, z, y, x, core)
        feat_out[i, 0] = sum(consts[r] * values[r] for r in range(3)) + consts[3]
        feat_out[i, 1] = sum(consts[4 + r] * values[r] for r in range(3)) + (
            consts[7] - (16 * served + 8).astype(F32)
        )
        for f, part in enumerate(conic_of(consts, symmetric(cov))):
            feat_out[i, 2 + f] = part
        feat_out[i, 5] = jnp.broadcast_to(log_sigmoid(values[10]), (8, 128))
        for c in range(3):
            feat_out[i, 6 + c] = 0.5 + sum(
                consts[8 + k] * values[11 + 3 * k + c] for k in range(16)
            )
        return carry

    lax.fori_loop(0, 4, serve, 0)


def three(x):
    high = x.astype(BF16).astype(F32)
    rest = x - high
    middle = rest.astype(BF16).astype(F32)
    return high, middle, rest - middle


def dot_nn(a, b):
    return lax.dot_general(a, b, (((1,), (0,)), ((), ())), preferred_element_type=F32)


def dot_nt(a, b):
    return lax.dot_general(a, b, (((1,), (1,)), ((), ())), preferred_element_type=F32)


def dot_tn(a, b):
    return lax.dot_general(a, b, (((0,), (0,)), ((), ())), preferred_element_type=F32)


CHUNK = 2048


def mark(list_ref, onehot):
    low_iota = lax.broadcasted_iota(jnp.int32, (256, 256), 0)

    def one(k, carry):
        cols = pl.ds(pl.multiple_of(k * 256, 256), 256)
        onehot[:, cols] = jnp.where(low_iota == (list_ref[:, cols] & 255), 1.0, 0.0).astype(BF16)
        return carry

    lax.fori_loop(0, 16, one, 0)


def composite(
    table_ref, list_ref, target_ref, basis_ref, basis_t_ref, rendered_out,
    onehot, feats, alpha, weight, weight_h, weight_m, colour_rows, image, grad_chunk, slot_acc,
):
    steps = CHUNK // 8
    chunks = 4096 // CHUNK
    table = table_ref[...].reshape(144, 256)
    table3 = jnp.concatenate(three(table), axis=0).astype(BF16)
    tile_of = lax.broadcasted_iota(jnp.int32, (1, CHUNK), 1) & 7
    in_tile = lax.broadcasted_iota(jnp.int32, (8, CHUNK), 0) == tile_of
    high_iota = lax.broadcasted_iota(jnp.int32, (16, CHUNK), 0)
    zeros_row = jnp.zeros((1, CHUNK), F32)
    image[...] = jnp.zeros_like(image)
    slot_acc[...] = jnp.zeros_like(slot_acc)

    def forward(k, through):
        cols = pl.ds(pl.multiple_of(k * CHUNK, CHUNK), CHUNK)
        index = list_ref[:, cols]
        picked = dot_nn(table3, onehot[:, cols])
        picked = picked[0:144] + picked[144:288] + picked[288:432]
        here = high_iota == (index >> 8)
        rows = [
            jnp.sum(jnp.where(here, picked[f * 16:(f + 1) * 16], 0.0), axis=0, keepdims=True)
            for f in range(9)
        ]
        u = rows[0] - (16 * tile_of + 8).astype(F32)
        v, a, b, c, log_opacity = rows[1:6]
        feats[0:1, cols] = u
        feats[1:2, cols] = v
        feats[2:3, cols] = a
        feats[3:4, cols] = b
        feats[4:5, cols] = c
        live = index >= 0
        along_u = a * u + b * v
        along_v = b * u + c * v
        constant = jnp.where(live, log_opacity - 0.5 * (along_u * u + along_v * v), -16384.0)
        terms = [constant, along_u, along_v, -0.5 * a, -b, -0.5 * c]
        terms = [t * LOG2E for t in terms] + [zeros_row, zeros_row]
        terms = jnp.concatenate(terms, axis=0)
        high, middle, low = three(terms)
        terms = jnp.concatenate([high, middle, low, jnp.zeros_like(low)], axis=0).astype(BF16)
        power = dot_tn(terms, basis_ref[...])
        seen = jnp.minimum(jnp.exp2(power), 0.99)
        alpha[cols, :] = seen
        for j in range(steps):
            one = seen[8 * j:8 * j + 8]
            weight[pl.ds(pl.multiple_of(k * CHUNK + 8 * j, 8), 8), :] = through * one
            through = through * (1.0 - one)
        part = weight[cols, :]
        part_h = part.astype(BF16)
        part_m = (part - part_h.astype(F32)).astype(BF16)
        weight_h[cols, :] = part_h
        weight_m[cols, :] = part_m
        masked = jnp.concatenate(
            [jnp.where(in_tile, rows[6 + ch], 0.0) for ch in range(3)], axis=0
        )
        high, middle, low = three(masked)
        stacked = jnp.concatenate([high, middle, high, jnp.zeros((8, CHUNK), F32)], axis=0).astype(BF16)
        colour_rows[:, cols] = stacked
        image[...] += dot_nn(stacked[0:48], part_h) + dot_nn(stacked[0:48], part_m)
        return through

    lax.fori_loop(0, chunks, forward, jnp.ones((8, 256), F32))
    picture = image[0:24] + image[24:48]
    rendered_out[...] = picture
    wrong = picture - target_ref[...]
    high, middle, low = three(wrong)
    wrong_q = jnp.concatenate([high, high, middle, jnp.zeros((8, 256), F32)], axis=0).astype(BF16)
    wrong_w = jnp.concatenate([high, middle], axis=0).astype(BF16)

    def backward(step, behind):
        k = chunks - 1 - step
        cols = pl.ds(pl.multiple_of(k * CHUNK, CHUNK), CHUNK)
        value = dot_tn(colour_rows[:, cols], wrong_q)
        for j in reversed(range(steps)):
            at = pl.ds(pl.multiple_of(k * CHUNK + 8 * j, 8), 8)
            seen = alpha[at, :]
            gain = value[8 * j:8 * j + 8] - behind
            grad_chunk[8 * j:8 * j + 8, :] = jnp.where(seen < 0.99, weight[at, :] * gain, 0.0)
            behind = behind * (1.0 - seen) + seen * value[8 * j:8 * j + 8]
        grad = grad_chunk[...]
        high = grad.astype(BF16)
        middle = (grad - high.astype(F32)).astype(BF16)
        basis_t = basis_t_ref[...]
        moments = dot_nt(basis_t, high) + dot_nt(basis_t, middle)
        tinted = dot_nt(wrong_w, weight_h[cols, :]) + dot_nt(wrong_w, weight_m[cols, :])
        tinted = tinted[0:24] + tinted[24:48]
        colour = [
            jnp.sum(jnp.where(in_tile, tinted[8 * ch:8 * ch + 8], 0.0), axis=0, keepdims=True)
            for ch in range(3)
        ]
        u, v, a, b, c = [feats[f:f + 1, cols] for f in range(5)]
        m1, mx, my, mxx, mxy, myy = [moments[f:f + 1] for f in range(6)]
        dx = mx - u * m1
        dy = my - v * m1
        found = [
            a * dx + b * dy,
            b * dx + c * dy,
            -0.5 * (mxx - u * (mx + dx)),
            -(mxy - u * my - v * dx),
            -0.5 * (myy - v * (my + dy)),
            m1,
        ] + colour
        found = jnp.concatenate(found + [zeros_row] * 7, axis=0)
        index = list_ref[:, cols]
        here = high_iota == (index >> 8)
        spread = [
            jnp.where(here, part[f:f + 1], 0.0) for part in three(found)[:2] for f in range(9)
        ]
        spread = jnp.concatenate(spread, axis=0).astype(BF16)
        slot_acc[...] += dot_nt(spread, onehot[:, cols])
        return behind

    lax.fori_loop(0, chunks, backward, jnp.zeros((8, 256), F32))
    total = slot_acc[0:144] + slot_acc[144:288]
    return total


def window_kernel(
    feat_ref, params_ref, consts_ref, ids_ref, list_ref, target_ref, basis_ref, basis_t_ref, mix_ref,
    rendered_out, grads_out,
    table, onehot, feats, alpha, weight, weight_h, weight_m, colour_rows,
    image, grad_chunk, slot_acc, leaving, got, gathered, acc,
    f_send, f_recv, b_send, b_recv, far_send, far_recv, near_send, near_recv,
):
    cell, view, z, y, x, core = place()
    greet_window(lambda: mark(list_ref, onehot))
    consts = [jnp.broadcast_to(consts_ref[:, k:k + 1], (8, 128)) for k in range(8)]
    down = lambda t: jnp.sum(t, axis=0, keepdims=True)

    def feature_copy(i, v):
        source, target = feat_ref.at[i, :, v, :], slot_window(table, cell)
        return Or_local(
            i + v, view,
            lambda: remote(
                source, target, f_send.at[i * 8 + v], f_recv.at[cell],
                requester(i, z, y, x, core), v,
            ),
            lambda: pltpu.make_async_copy(source, target, f_recv.at[cell]),
        )

    for i in (2, 1, 3, 0):
        for v in range(8):
            feature_copy(i, v).start()

    def arrived(owner, carry):
        pltpu.make_async_copy(
            feat_ref.at[0, :, 0, :], slot_window(table, owner), f_recv.at[owner]
        ).wait()
        return carry

    lax.fori_loop(0, 32, arrived, 0)

    total = composite(
        table, list_ref, target_ref, basis_ref, basis_t_ref, rendered_out,
        onehot, feats, alpha, weight, weight_h, weight_m, colour_rows, image, grad_chunk, slot_acc,
    )
    leaving[...] = total.reshape(9, 16, 256)

    def grad_copy(n):
        owner, who, i = owner_at(OFFSETS[n], z, y)
        source, target = slot_window(leaving, owner), got.at[i, :, view, :]
        return Or_local(
            31 - n, view,
            lambda: remote(source, target, b_send.at[n], b_recv.at[i * 8 + view], owner, who),
            lambda: pltpu.make_async_copy(source, target, b_recv.at[i * 8 + view]),
        )

    for n in range(32):
        grad_copy(n).start()
    for i in range(4):
        for v in range(8):
            feature_copy(i, v).wait_send()
    acc[...] = jnp.zeros_like(acc)

    def far(step, i):
        who = (view + 2 * step) & 7
        return remote(
            gathered.at[view, i], gathered.at[view, i], far_send.at[step, i], far_recv.at[step, i],
            cell, who,
        )

    def near(step, i):
        which = (view - 2 * step) & 7
        return remote(
            gathered.at[which, i], gathered.at[which, i],
            near_send.at[step, i], near_recv.at[step, i], cell, view ^ 1,
        )

    values = [
        jnp.concatenate([params_ref[i, k:k + 1] for i in range(4)], axis=1) for k in range(11)
    ]
    all_scales, all_turns, all_norm, all_inverse, turned = rotation_of(values)
    all_scaled = [turned[r][k] * all_scales[k] for r in range(3) for k in range(3)]
    all_faint = 1.0 / (1.0 + jnp.exp(values[10]))
    zero = jnp.zeros((1, 128), F32)
    order = (0, 3, 1, 2)
    for i in order:
        for v in range(8):
            pltpu.make_async_copy(
                slot_window(leaving, cell), got.at[i, :, v, :], b_recv.at[i * 8 + v]
            ).wait()
        a, b, c = [feat_ref[i, f] for f in range(2, 5)]
        du, dv, da, db, dc, dlog = [got[i, f] for f in range(6)]
        position = [down(consts[r] * du + consts[4 + r] * dv) for r in range(3)]
        half = 0.5 * db
        p00 = a * da + b * half
        p01 = a * half + b * dc
        p10 = b * da + c * half
        p11 = b * half + c * dc
        s00 = -(p00 * a + p01 * b)
        s01 = -(p00 * b + p01 * c)
        s11 = -(p10 * b + p11 * c)
        first = [consts[r] * s00 + consts[4 + r] * s01 for r in range(3)]
        second = [consts[r] * s01 + consts[4 + r] * s11 for r in range(3)]
        cov = [down(first[r] * consts[t] + second[r] * consts[4 + t]) for r, t in PAIRS]
        lanes = slice(128 * i, 128 * i + 128)
        scales, (qw, qx, qy, qz), scaled = [
            [t[:, lanes] for t in group] for group in (all_scales, all_turns, all_scaled)
        ]
        scaled = [scaled[3 * r:3 * r + 3] for r in range(3)]
        inverse, faint = all_inverse[:, lanes], all_faint[:, lanes]
        cov = symmetric(cov)
        dscaled = [
            [2.0 * sum(cov[r][t] * scaled[t][k] for t in range(3)) for k in range(3)]
            for r in range(3)
        ]
        dlogs = [sum(dscaled[r][k] * scaled[r][k] for r in range(3)) for k in range(3)]
        (e00, e01, e02), (e10, e11, e12), (e20, e21, e22) = [
            [dscaled[r][k] * scales[k] for k in range(3)] for r in range(3)
        ]
        qd = [
            2.0 * (qz * (e10 - e01) + qy * (e02 - e20) + qx * (e21 - e12)),
            2.0 * (qy * (e01 + e10) + qz * (e02 + e20) + qw * (e21 - e12) - 2.0 * qx * (e11 + e22)),
            2.0 * (qx * (e01 + e10) + qw * (e02 - e20) + qz * (e12 + e21) - 2.0 * qy * (e00 + e22)),
            2.0 * (qw * (e10 - e01) + qx * (e02 + e20) + qy * (e12 + e21) - 2.0 * qz * (e00 + e11)),
        ]
        inward = jnp.where(all_norm[:, lanes] > 0.5, qw * qd[0] + qx * qd[1] + qy * qd[2] + qz * qd[3], 0.0)
        dq = [(g - q * inward) * inverse for g, q in zip(qd, (qw, qx, qy, qz))]
        dlogit = down(dlog) * faint
        name = ids_ref[i:i + 1].astype(F32)
        rows = position + dlogs + dq + [dlogit, name] + [zero] * 4
        gathered[view, i, 0:16] = jnp.concatenate(rows, axis=0)
        for ch in range(3):
            gathered[view, i, 16 + 8 * ch:24 + 8 * ch] = got[i, 6 + ch]
        for step in (2, 1, 3):
            far(step, i).start()
        near(0, i).start()

    def far_came(step, i):
        which = (view - 2 * step) & 7
        pltpu.make_async_copy(
            gathered.at[view, i], gathered.at[which, i], far_recv.at[step, i]
        ).wait()
        near(step, i).start()

    def near_came(step):
        which = ((view ^ 1) - 2 * step) & 7
        for i in order:
            pltpu.make_async_copy(
                gathered.at[view, i], gathered.at[which, i], near_recv.at[step, i]
            ).wait()
        return which

    base = (view * 4096).astype(F32)
    low_iota = lax.broadcasted_iota(jnp.int32, (256, 512), 0)

    def deposit(which):
        block = jnp.concatenate([gathered[which, i] for i in range(4)], axis=1)
        name = (block[11:12] - base).astype(jnp.int32)
        hot = jnp.where(low_iota == (name & 255), 1.0, 0.0).astype(BF16)
        row = name >> 8
        parts = jnp.concatenate(three(block)[:2], axis=0)
        spread = [jnp.where(row == h, parts, 0.0).astype(BF16) for h in range(16)]
        acc[...] += dot_nt(jnp.concatenate(spread, axis=0), hot)

    deposit(view)
    for n in range(32):
        grad_copy(n).wait_send()
    for i in order:
        far_came(1, i)
        far_came(3, i)
    deposit(near_came(0))
    for i in order:
        far_came(2, i)
    for step in (1, 3, 2):
        deposit((view - 2 * step) & 7)
    for i in range(4):
        for step in (1, 2, 3):
            far(step, i).wait_send()
        near(0, i).wait_send()
    for step in (1, 3, 2):
        deposit(near_came(step))

    mix = mix_ref[...].T[0:59]
    for h in range(16):
        at = 80 * h
        grads_out[:, h * 256:(h + 1) * 256] = jnp.dot(
            mix, acc[at:at + 40] + acc[at + 40:at + 80],
            precision=lax.Precision.HIGHEST, preferred_element_type=F32,
        )
    for i in range(4):
        for step in (1, 3, 2):
            near(step, i).wait_send()


def pixel_basis():
    pixel = np.arange(256)
    x = pixel % 16 - 7.5
    y = pixel // 16 - 7.5
    eight = np.stack([np.ones(256), x, y, x * x, x * y, y * y, 0 * x, 0 * x])
    wide = np.concatenate([eight, eight, eight, 0 * eight]).astype(np.float32)
    tall = np.concatenate([eight, 0 * eight]).astype(np.float32)
    return jnp.asarray(wide, BF16), jnp.asarray(tall, BF16)


VM = pl.BlockSpec(memory_space=pltpu.VMEM)
SM = pl.BlockSpec(memory_space=pltpu.SMEM)
MIB = 1024 * 1024
DMA = pltpu.SemaphoreType.DMA


def shape(*dims, dtype=F32):
    return jax.ShapeDtypeStruct(dims, dtype)


def ask(camera, ids, gaussians):
    return pl.pallas_call(
        ask_kernel,
        out_shape=(shape(4, 128, dtype=jnp.int32), shape(8, 128), shape(59, 32768)),
        in_specs=[VM, VM, pl.BlockSpec(memory_space=pltpu.HBM)],
        out_specs=(VM, VM, pl.BlockSpec(memory_space=pl.ANY)),
        scratch_shapes=[
            DMA,
            pltpu.VMEM((1, 128), F32),
            pltpu.VMEM((8, 128), F32),
            pltpu.VMEM((4, 128), jnp.int32),
            DMA, DMA((4,)), DMA((4,)), DMA((8,)), DMA((8,)),
        ],
        compiler_params=pltpu.CompilerParams(
            collective_id=0, has_side_effects=True, vmem_limit_bytes=44 * MIB
        ),
        name="ask",
    )(camera, ids, gaussians)


def project(ids, cams, gaussians):
    return pl.pallas_call(
        project_kernel,
        out_shape=(shape(4, 9, 8, 128), shape(4, 16, 128), shape(8, 128), shape(40, 128)),
        in_specs=[SM, VM, VM],
        out_specs=(VM, VM, VM, VM),
        scratch_shapes=[pltpu.VMEM((64, 128), F32)],
        compiler_params=pltpu.CompilerParams(vmem_limit_bytes=16 * MIB),
        name="project",
    )(ids, cams, gaussians)


def window(feat, params, consts, ids, listed, target, mix):
    wide, tall = pixel_basis()
    return pl.pallas_call(
        window_kernel,
        out_shape=(shape(24, 256), shape(59, 4096)),
        in_specs=[VM] * 9,
        out_specs=(VM, VM),
        scratch_shapes=[
            pltpu.VMEM((9, 16, 256), F32),
            pltpu.VMEM((256, 4096), BF16),
            pltpu.VMEM((8, 4096), F32),
            pltpu.VMEM((4096, 256), F32),
            pltpu.VMEM((4096, 256), F32),
            pltpu.VMEM((4096, 256), BF16),
            pltpu.VMEM((4096, 256), BF16),
            pltpu.VMEM((80, 4096), BF16),
            pltpu.VMEM((48, 256), F32),
            pltpu.VMEM((CHUNK, 256), F32),
            pltpu.VMEM((288, 256), F32),
            pltpu.VMEM((9, 16, 256), F32),
            pltpu.VMEM((4, 9, 8, 128), F32),
            pltpu.VMEM((8, 4, 40, 128), F32),
            pltpu.VMEM((1280, 256), F32),
            DMA((32,)), DMA((32,)), DMA((32,)), DMA((32,)),
            DMA((4, 4)), DMA((4, 4)), DMA((4, 4)), DMA((4, 4)),
        ],
        compiler_params=pltpu.CompilerParams(
            collective_id=1, has_side_effects=True, vmem_limit_bytes=48 * MIB
        ),
        name="window",
    )(feat, params, consts, ids, listed, target, wide, tall, mix)


def on_device(gaussians, cameras, fetch_ids, tile_lists, lengths, target_image):
    live = jnp.arange(512, dtype=jnp.int32)[:, None] < lengths[None, :]
    listed = jnp.where(live, tile_lists[0].T, -1).reshape(1, 4096)
    target = target_image.reshape(24, 256)
    ids, cams, table = ask(cameras, fetch_ids[0], gaussians)
    feat, params, consts, mix = project(ids, cams, table)
    picture, param_grads = window(feat, params, consts, ids, listed, target, mix)
    return picture.reshape(3, 1, 8, 256), param_grads


def solution(mesh):
    in_specs = (
        P(None, "cell"),
        P("view", None),
        P("cell", None, None),
        P("view", "cell", None),
        P("cell"),
        P(None, "view", "cell", None),
    )
    out_specs = (P(None, "view", "cell", None), P(None, ("cell", "view")))
    return jax.shard_map(
        on_device, mesh=mesh, in_specs=in_specs, out_specs=out_specs, check_vma=False
    )
```
